128 devices in a mesh: section: 4 (over y), fsdp: 32 (over x, z, core).
Axes of the slice: x: 4, y: 4, z: 4, core: 2. Of those that a mesh axis runs over, the one named last changes fastest.
Arguments:
- weights: bfloat16 [4, 4096, 4096], P('section', 'fsdp'), may hold values from -0.09375 to 0.09375
- kv_weights: bfloat16 [4, 4096, 256], P('section', 'fsdp'), may hold values from -0.09375 to 0.09375
- gammas: float32 [4, 3], P('section'), may hold values from 1 to 3
- gains: bfloat16 [4, 4096], P('section'), may hold values from 0.5 to 1.5
- starts: bfloat16 [4, 3, 4096], P('section', None, 'fsdp'), may hold values from -6 to 6
- source: bfloat16 [2, 32, 128, 4096], P(None, 'fsdp'), may hold values from -6 to 6
- target: bfloat16 [2, 32, 128, 4096], P(None, 'fsdp'), may hold values from -6 to 6
- lengths: int32 [2, 32], P(None, 'fsdp'), may hold values from 32 to 128, as said below
Outputs:
- states: bfloat16 [4, 2, 32, 128, 4096], P('section', None, 'fsdp')
- next_starts: float32 [4, 3, 4096], P('section', None, 'fsdp')
The draws below stay inside these ranges and needn't reach their ends.
Inputs may be any that keep to these rules, and one draw needn't show every extreme that they name: `lengths`: key positions at or beyond a sequence's length are padding; some sequence has all 128 tokens.
All inputs are finite; a program needn't handle non-finite values.
Results may differ from the reference program's by a relative error of at most 0.024.
Values may be sent and summed in bfloat16 or wider, within the bound.
No kernel may reach another device: no remote copies, remote signals or barrier semaphores. Data moves between devices by JAX's collectives and lax.ppermute only.
A program may use at most 192 MiB of HBM per device.

```python
import math
import jax
import jax.numpy as jnp
from jax import lax

D = 4096
HEAD = 128
MICRO = 2
SEQ_LEN = 128
SEQ_DEV = 1
SEQS = 32
N_SECTION = 4
N_FSDP = 32


def draw_lengths(key, part):
    key = jax.random.fold_in(key, 11)
    drawn = jax.random.randint(key, (MICRO, SEQ_DEV * N_FSDP), SEQ_LEN // 4, SEQ_LEN + 1, dtype=jnp.int32)
    return drawn.at[0, 0].set(SEQ_LEN)


def levels(stream_key, shape, pieces, low, largest):
    level, own = 1.0, jax.random.fold_in(stream_key, 6)
    for axis_at, blocks in pieces:
        steps = jnp.exp(jax.random.uniform(jax.random.fold_in(own, axis_at), (blocks,), jnp.float32, low / len(pieces), largest / len(pieces)))
        level = level * jnp.repeat(steps, shape[axis_at] // blocks).reshape([-1 if axis == axis_at else 1 for axis in range(len(shape))])
    return level


def noise(key, shape, scale, reach, shards=(), kind=jnp.bfloat16):
    values = scale * jax.random.normal(key, shape, jnp.float32)
    if shards:
        values = values * levels(key, shape, shards, -0.22, 0.18)
    return jnp.clip(values, -reach, reach).astype(kind)


def setup_inputs(seed: int = 0) -> dict:
    arg_keys = jax.random.split(jax.random.key(seed), 9)
    return {
        "weights": noise(arg_keys[0], (N_SECTION, D, D), D ** -0.5, 0.09375, ((0, 4), (1, 32))),
        "kv_weights": noise(arg_keys[1], (N_SECTION, D, 2 * HEAD), D ** -0.5, 0.09375, ((0, 4), (1, 32))),
        "gammas": jnp.clip(jnp.exp(math.log(3.0) - 1.0986123 * jax.random.uniform(arg_keys[2], (N_SECTION, 3), jnp.float32) ** levels(arg_keys[2], (N_SECTION, 3), ((0, 4),), -0.2, 0.2)), 1.0, 3.0),
        "gains": jnp.clip(1.0 + 0.1 * jax.random.normal(arg_keys[3], (N_SECTION, D), jnp.float32), 0.5, 1.5).astype(jnp.bfloat16),
        "starts": noise(arg_keys[4], (N_SECTION, 3, D), 1.0, 6.0, ((0, 4), (2, 32))),
        "source": noise(arg_keys[5], (MICRO, SEQS, SEQ_LEN, D), 1.0, 6.0, ((1, 32),)),
        "target": noise(arg_keys[6], (MICRO, SEQS, SEQ_LEN, D), 1.0, 6.0, ((1, 32),)),
        "lengths": draw_lengths(jax.random.fold_in(arg_keys[8], 71), 0),
    }


EPS = 1e-06

def normalize_rows(values):
    return values * lax.rsqrt(lax.optimization_barrier(jnp.mean(values * values, axis=-1, keepdims=True)) + EPS)

def attention_layer(states, memory, weight, kv_weight, scales, gain, seq_lengths):
    seqs, length, width = states.shape
    heads = width // HEAD
    residual = states.astype(jnp.float32)
    gain_wide = gain.astype(jnp.float32)
    normed = (normalize_rows(residual) * gain_wide).astype(jnp.bfloat16)
    memory_normed = (normalize_rows(memory.astype(jnp.float32)) * gain_wide).astype(jnp.bfloat16)
    query = (jnp.dot(normed.reshape(seqs * length, width), weight, preferred_element_type=jnp.float32) * scales[0]).astype(jnp.bfloat16)
    projected = jnp.dot(memory_normed.reshape(seqs * length, width), kv_weight, preferred_element_type=jnp.float32)
    keys = (projected[:, :HEAD] * scales[1]).astype(jnp.bfloat16)
    values = (projected[:, HEAD:] * scales[2]).astype(jnp.bfloat16)
    query = query.reshape(seqs, length, heads, HEAD).astype(jnp.float32)
    keys = keys.reshape(seqs, length, HEAD).astype(jnp.float32)
    values = values.reshape(seqs, length, HEAD).astype(jnp.float32)
    scores = jnp.einsum('sqhe,ske->shqk', query, keys) / math.sqrt(HEAD)
    positions = jnp.arange(length, dtype=jnp.int32)
    valid = positions[None, :] < seq_lengths[:, None].astype(jnp.int32)
    expd = jnp.where(valid[:, None, None, :], jnp.exp(scores), 0.0)
    probs = (expd / lax.optimization_barrier(jnp.sum(expd, axis=-1, keepdims=True))).astype(jnp.bfloat16)
    context = jnp.einsum('shqk,ske->sqhe', probs.astype(jnp.float32), values)
    return (residual + context.reshape(seqs, length, width)).astype(jnp.bfloat16)

def spectral(matrix, start, gamma):
    along = jnp.dot(start, matrix, preferred_element_type=jnp.float32)
    direction = (along * lax.rsqrt(jnp.sum(along * along) + EPS)).astype(jnp.bfloat16)
    image = jnp.dot(matrix, direction, preferred_element_type=jnp.float32)
    sigma = jnp.sqrt(jnp.sum(image * image) + EPS)
    return (gamma / sigma, image / sigma)

def reference(weights, kv_weights, gammas, gains, starts, source, target, lengths):
    scales = []
    updated = []
    for layer in range(N_SECTION):
        matrices = (weights[layer], kv_weights[layer][:, :HEAD], kv_weights[layer][:, HEAD:])
        layer_scales = []
        layer_fresh = []
        for column in range(3):
            scale, fresh = spectral(matrices[column], starts[layer, column], gammas[layer, column])
            layer_scales.append(scale)
            layer_fresh.append(fresh)
        scales.append(jnp.stack(layer_scales))
        updated.append(jnp.stack(layer_fresh))
    half = N_SECTION // 2
    results = [[None] * MICRO for layer in range(N_SECTION)]
    for batch in range(MICRO):
        current = source[batch]
        memory = current
        for layer in range(N_SECTION):
            if layer == half:
                current = target[batch]
            keyed = current if layer < half else memory
            current = attention_layer(current, keyed, weights[layer], kv_weights[layer], scales[layer], gains[layer], lengths[batch])
            if layer == half - 1:
                memory = current
            results[layer][batch] = current
    states = jnp.stack([jnp.stack(results[layer]) for layer in range(N_SECTION)])
    return (states, jnp.stack(updated))
```

```python
import functools
import math

import jax
import jax.numpy as jnp
from jax import lax
from jax.experimental import pallas as pl
from jax.experimental.pallas import tpu as pltpu
from jax.sharding import PartitionSpec as P

HEAD = 128
EPS = 1e-06
F32 = jnp.float32
BF16 = jnp.bfloat16
VMEM_LIMIT = 48 * 1024 * 1024
BLOCK = 512
ROUTE = (0, -1, 1, 2)


def dot(a, b):
    return jnp.dot(a, b, preferred_element_type=F32)


def moves(fn):
    pairs = []
    for index in range(32):
        x, z, core = index // 8, (index // 2) % 4, index % 2
        x2, z2, core2 = fn(x, z, core)
        pairs.append((index, (x2 % 4) * 8 + (z2 % 4) * 2 + core2))
    return pairs


def first_move(step):
    return moves(lambda x, z, c: (x, z + step, c) if c == 0 else (x + step, z, c))


def second_move(step):
    return moves(lambda x, z, c: (x + step, z, c) if c == 0 else (x, z + step, c))


CORE_SWAP = moves(lambda x, z, c: (x, z, 1 - c))


def send(value, pairs):
    return lax.ppermute(value, "fsdp", pairs)


def ring(block, move):
    half = block.shape[0] // 2
    before = send(block, move(1))
    after = send(block, move(-1))
    far_low = send(before[:half], move(1))
    far_high = send(after[half:], move(-1))
    return [block, before, after, far_low, far_high]


def gather(block):
    line = jnp.concatenate(ring(block, first_move), 0)
    own = jnp.concatenate(ring(line, second_move), 0)
    return own, send(own, CORE_SWAP)


def row_order():
    index = lax.axis_index("fsdp")
    x, z, core = index // 8, (index // 2) % 4, index % 2
    first = jnp.array(ROUTE, jnp.int32)
    line = jnp.tile(first, 4)
    plane = jnp.repeat(first, 4)

    def order(kind):
        zs = z + jnp.where(kind == 0, line, plane)
        xs = x + jnp.where(kind == 0, plane, line)
        return ((xs + 8) % 4) * 8 + ((zs + 8) % 4) * 2 + kind

    return jnp.concatenate([order(core), order(1 - core)]).astype(jnp.int32)


def total(value):
    value = value + send(value, CORE_SWAP)
    for along_x in (False, True):
        parts = [
            send(value, moves(lambda x, z, c, s=s: (x + s, z, c) if along_x else (x, z + s, c)))
            for s in (1, -1, 2)
        ]
        value = value + parts[0] + parts[1] + parts[2]
    return value


def norm_kernel(order_ref, x_ref, gain_ref, out_ref):
    wide = x_ref[...].astype(F32)
    inv = lax.rsqrt(jnp.mean(wide * wide, axis=-1, keepdims=True) + EPS)
    for k in range(32):
        at = pl.ds(pl.multiple_of(order_ref[k] * 128, 128), 128)
        part = x_ref[:, at].astype(F32) * inv * gain_ref[:, at]
        out_ref[:, k * 128 : (k + 1) * 128] = part.astype(BF16)


def norm_rows(x, gain, order):
    rows, width = x.shape
    return pl.pallas_call(
        norm_kernel,
        out_shape=jax.ShapeDtypeStruct((rows, width), BF16),
        in_specs=[
            pl.BlockSpec(memory_space=pltpu.SMEM),
            pl.BlockSpec(memory_space=pltpu.VMEM),
            pl.BlockSpec(memory_space=pltpu.VMEM),
        ],
        out_specs=pl.BlockSpec(memory_space=pltpu.VMEM),
        compiler_params=pltpu.CompilerParams(vmem_limit_bytes=VMEM_LIMIT),
        cost_estimate=pl.CostEstimate(flops=4 * rows * width, bytes_accessed=4 * rows * width, transcendentals=0),
    )(order, x, gain.astype(F32).reshape(1, width))


def attend(q, k_ref, v_ref, resid_ref, lengths_ref, out_ref):
    seqs = q.shape[0] // 128
    heads = q.shape[1] // HEAD
    position = lax.broadcasted_iota(jnp.int32, (128, 128), 1)
    for m in range(seqs):
        rows = slice(m * 128, (m + 1) * 128)
        keys = k_ref[rows, :]
        values = v_ref[rows, :]
        valid = position < lengths_ref[m]
        for h in range(heads):
            cols = slice(h * HEAD, (h + 1) * HEAD)
            scores = lax.dot_general(
                q[rows, cols], keys, (((1,), (1,)), ((), ())), preferred_element_type=F32
            ) * (1.0 / math.sqrt(HEAD))
            expd = jnp.where(valid, jnp.exp(scores), 0.0)
            probs = (expd / jnp.sum(expd, axis=-1, keepdims=True)).astype(BF16)
            out = resid_ref[rows, cols].astype(F32) + dot(probs, values)
            out_ref[rows, cols] = out.astype(BF16)


def layer_kernel(lengths_ref, mode_ref, scale_ref, xn_ref, wa_ref, wb_ref, k_ref, v_ref, resid_ref, out_ref):
    half = wa_ref.shape[0]
    acc = dot(xn_ref[:, :half], wa_ref[...]) + dot(xn_ref[:, half:], wb_ref[...])
    q = (acc * scale_ref[0]).astype(BF16)

    @pl.when(mode_ref[0] == 0)
    def _():
        attend(q, k_ref, v_ref, resid_ref, lengths_ref, out_ref)

    @pl.when(mode_ref[0] != 0)
    def _():
        out_ref[...] = q


def layer_part(xn, own, other, keys, values, resid, part, width, lengths, scale, mode):
    rows = xn.shape[0]
    depth = own.shape[0]
    steps = width // BLOCK
    first = part // BLOCK
    smem = pl.BlockSpec(memory_space=pltpu.SMEM)
    whole = lambda shape: pl.BlockSpec(shape, lambda j: (0, 0))
    return pl.pallas_call(
        layer_kernel,
        grid=(steps,),
        out_shape=jax.ShapeDtypeStruct((rows, width), BF16),
        in_specs=[
            smem,
            smem,
            smem,
            whole(xn.shape),
            pl.BlockSpec((depth, BLOCK), lambda j: (0, j)),
            pl.BlockSpec((depth, BLOCK), lambda j: (0, j)),
            whole(keys.shape),
            whole(values.shape),
            pl.BlockSpec((rows, BLOCK), lambda j: (0, first + j)),
        ],
        out_specs=pl.BlockSpec((rows, BLOCK), lambda j: (0, j)),
        compiler_params=pltpu.CompilerParams(vmem_limit_bytes=VMEM_LIMIT),
        cost_estimate=pl.CostEstimate(
            flops=4 * rows * depth * width, bytes_accessed=4 * depth * width, transcendentals=rows * width
        ),
    )(lengths, mode, scale, xn, own, other, keys, values, resid)


def attention_kernel(lengths_ref, q_ref, k_ref, v_ref, resid_ref, out_ref):
    attend(q_ref[...], k_ref, v_ref, resid_ref, lengths_ref, out_ref)


def attention(q, keys, values, resid, lengths):
    rows, width = q.shape
    block = pl.BlockSpec((rows, BLOCK), lambda j: (0, j))
    whole = pl.BlockSpec(keys.shape, lambda j: (0, 0))
    return pl.pallas_call(
        attention_kernel,
        grid=(width // BLOCK,),
        out_shape=jax.ShapeDtypeStruct((rows, width), BF16),
        in_specs=[pl.BlockSpec(memory_space=pltpu.SMEM), block, whole, whole, block],
        out_specs=block,
        compiler_params=pltpu.CompilerParams(vmem_limit_bytes=VMEM_LIMIT),
        cost_estimate=pl.CostEstimate(
            flops=4 * rows * 128 * width, bytes_accessed=6 * rows * width, transcendentals=rows * width
        ),
    )(lengths, q, keys, values, resid)


def unit_direction(along):
    return (along * lax.rsqrt(jnp.sum(along * along) + EPS)).astype(BF16)


def spectral(weight, kv_part, start_rows, gamma):
    width = weight.shape[1]
    parts = jnp.concatenate(
        [
            dot(start_rows[0:1], weight)[0],
            dot(start_rows[1:2], kv_part[:, :HEAD])[0],
            dot(start_rows[2:3], kv_part[:, HEAD:])[0],
        ]
    )
    along = total(parts.reshape(-1, 128)).reshape(-1)
    images = jnp.stack(
        [
            dot(weight, unit_direction(along[:width])),
            dot(kv_part[:, :HEAD], unit_direction(along[width : width + HEAD])),
            dot(kv_part[:, HEAD:], unit_direction(along[width + HEAD :])),
        ]
    )
    squares = jnp.sum(images * images, axis=1)
    totals = total(jnp.broadcast_to(squares[:, None], (3, 128)))[:, 0]
    sigmas = jnp.sqrt(totals + EPS)
    return gamma / sigmas, images / sigmas[:, None]


def project(xn, own, other, key_scale, value_scale):
    half = own.shape[0]
    projected = dot(xn[:, :half], own) + dot(xn[:, half:], other)
    return (projected[:, :HEAD] * key_scale).astype(BF16), (projected[:, HEAD:] * value_scale).astype(BF16)


def shards(weights, kv_weights, gammas, gains, starts, source, target, lengths):
    weight, kv_part, gamma, gain, start_rows = weights[0], kv_weights[0], gammas[0], gains[0], starts[0]
    width = weight.shape[1]
    section = lax.axis_index("section")
    micro, seqs, length, _ = source.shape
    rows = micro * seqs * length
    seq_lengths = lengths.reshape(-1)
    source2 = source.reshape(rows, width)
    target2 = target.reshape(rows, width)

    hop = lambda value, pairs: lax.ppermute(value, "section", pairs)
    scales, next_part = spectral(weight, kv_part, start_rows, gamma)
    order = row_order()

    entering = jnp.where(section == 2, target2, source2)
    xn = norm_rows(entering, gain, order)

    part_width = 1024
    parts = [weight[:, at : at + part_width] for at in range(0, width, part_width)]
    parts[0] = jnp.concatenate([parts[0], kv_part], 1)
    gathered = [gather(part) for part in parts]
    kv_own, kv_other = (half[:, part_width:] for half in gathered[0])

    kv2_own = hop(kv_own, [(2, 1)])
    kv3_own = hop(kv_own, [(3, 1)])
    kv2_other = send(kv2_own, CORE_SWAP)
    kv3_other = send(kv3_own, CORE_SWAP)
    small = jnp.concatenate([gain.astype(F32), jnp.pad(scales, (0, 125))]).reshape(-1, 128)
    small2 = hop(small, [(2, 1)]).reshape(-1)
    small3 = hop(small, [(3, 1)]).reshape(-1)

    scale0 = scales[0:1]
    mode = jnp.where(section == 2, 1, 0).astype(jnp.int32).reshape(1)
    keys, values = project(xn, kv_own, kv_other, scales[1], scales[2])
    first, passed = [], []
    for j, (own, other) in enumerate(gathered):
        made = layer_part(
            xn, own, other, keys, values, entering, j * part_width, part_width, seq_lengths, scale0, mode
        )
        first.append(made)
        passed.append(hop(made, [(0, 1), (2, 3)]))
    first = jnp.concatenate(first, 1)
    passed = jnp.concatenate(passed, 1)

    def whole_layer(x, xn, keys, values):
        zero = jnp.zeros((1,), jnp.int32)
        return jnp.concatenate(
            [
                layer_part(xn, own, other, keys, values, x, j * part_width, part_width, seq_lengths, scale0, zero)
                for j, (own, other) in enumerate(gathered)
            ],
            1,
        )

    def encoder_end():
        xn1 = norm_rows(passed, gain, order)
        keys1, values1 = project(xn1, kv_own, kv_other, scales[1], scales[2])
        out = whole_layer(passed, xn1, keys1, values1)
        made = []
        for own, other, extra in ((kv2_own, kv2_other, small2), (kv3_own, kv3_other, small3)):
            memory = norm_rows(out, extra[:width], order)
            made += project(memory, own, other, extra[width + 1], extra[width + 2])
        return out, jnp.concatenate(made, 1)

    def encoder_skip():
        return jnp.zeros((rows, width), BF16), jnp.zeros((rows, 4 * HEAD), BF16)

    out1, cross = lax.cond(section == 1, encoder_end, encoder_skip)
    cross = hop(cross, [(1, 2)]) + hop(cross, [(1, 3)])

    query2 = jnp.where(section == 2, first, passed)

    def decoder():
        out2 = attention(query2, cross[:, :HEAD], cross[:, HEAD : 2 * HEAD], target2, seq_lengths)

        def last():
            xn3 = norm_rows(out2, gain, order)
            return whole_layer(out2, xn3, cross[:, 2 * HEAD : 3 * HEAD], cross[:, 3 * HEAD :])

        return lax.cond(section == 3, last, lambda: out2)

    def encoder():
        return jnp.where(section == 0, first, out1)

    result = lax.cond(section >= 2, decoder, encoder)
    return result.reshape(1, micro, seqs, length, width), next_part[None]


def solution(mesh):
    in_specs = (
        P("section", "fsdp", None),
        P("section", "fsdp", None),
        P("section", None),
        P("section", None),
        P("section", None, "fsdp"),
        P(None, "fsdp", None, None),
        P(None, "fsdp", None, None),
        P(None, "fsdp"),
    )
    out_specs = (P("section", None, "fsdp", None, None), P("section", None, "fsdp"))
    return jax.shard_map(shards, mesh=mesh, in_specs=in_specs, out_specs=out_specs, check_vma=False)
```

```python
import functools
import math

import jax
import jax.numpy as jnp
from jax import lax
from jax.experimental import pallas as pl
from jax.experimental.pallas import tpu as pltpu
from jax.sharding import PartitionSpec as P

HEAD = 128
EPS = 1e-06
F32 = jnp.float32
BF16 = jnp.bfloat16
VMEM_LIMIT = 48 * 1024 * 1024
BLOCK = 512
ROUTE = (0, -1, 1, 2)
PARTS = (1024, 1024, 1024, 1024)
SLOTS = 3
LOG2E_SCALED = math.log2(math.e) / math.sqrt(HEAD)
ANY = pl.BlockSpec(memory_space=pl.ANY)
VMEM = pl.BlockSpec(memory_space=pltpu.VMEM)
SMEM = pl.BlockSpec(memory_space=pltpu.SMEM)


def dot(a, b):
    return jnp.dot(a, b, preferred_element_type=F32)


def moves(fn):
    pairs = []
    for index in range(32):
        x, z, core = index // 8, (index // 2) % 4, index % 2
        x2, z2, core2 = fn(x, z, core)
        pairs.append((index, (x2 % 4) * 8 + (z2 % 4) * 2 + core2))
    return pairs


def first_move(step):
    return moves(lambda x, z, c: (x, z + step, c) if c == 0 else (x + step, z, c))


def second_move(step):
    return moves(lambda x, z, c: (x + step, z, c) if c == 0 else (x, z + step, c))


CORE_SWAP = moves(lambda x, z, c: (x, z, 1 - c))
DOUBLING = (
    CORE_SWAP,
    moves(lambda x, z, c: (x, z ^ 1, c)),
    moves(lambda x, z, c: (x ^ 1, z, c)),
    moves(lambda x, z, c: (x, z ^ 2, c)),
    moves(lambda x, z, c: (x ^ 2, z, c)),
)


def send(value, pairs):
    return lax.ppermute(value, "fsdp", pairs)


def ring(block, move, forward):
    before = send(block, move(1))
    after = send(block, move(-1))
    far = send(before, move(1)) if forward else send(after, move(-1))
    return [block, before, after, far]


def row_order():
    index = lax.axis_index("fsdp")
    x, z, core = index // 8, (index // 2) % 4, index % 2
    first = jnp.array(ROUTE, jnp.int32)
    line = jnp.tile(first, 4)
    plane = jnp.repeat(first, 4)

    def order(kind):
        zs = z + jnp.where(kind == 0, line, plane)
        xs = x + jnp.where(kind == 0, plane, line)
        return ((xs + 8) % 4) * 8 + ((zs + 8) % 4) * 2 + kind

    return jnp.concatenate([order(core), order(1 - core)]).astype(jnp.int32)


def total(value):
    for pairs in DOUBLING:
        value = value + send(value, pairs)
    return value


def params():
    return pltpu.CompilerParams(vmem_limit_bytes=VMEM_LIMIT)


def cost(flops, size, exps=0):
    return pl.CostEstimate(flops=int(flops), bytes_accessed=int(size), transcendentals=int(exps))


def stack_kernel(count, *refs):
    sources, out, sems = refs[:count], refs[count], refs[count + 1]
    rows = sources[0].shape[0]
    copies = [
        pltpu.make_async_copy(source, out.at[pl.ds(i * rows, rows)], sems.at[i])
        for i, source in enumerate(sources)
    ]
    for copy in copies:
        copy.start()
    for copy in copies:
        copy.wait()


def stack(blocks):
    count = len(blocks)
    rows, width = blocks[0].shape
    return pl.pallas_call(
        functools.partial(stack_kernel, count),
        out_shape=jax.ShapeDtypeStruct((count * rows, width), blocks[0].dtype),
        in_specs=[ANY] * count,
        out_specs=ANY,
        scratch_shapes=[pltpu.SemaphoreType.DMA((count,))],
        compiler_params=pltpu.CompilerParams(vmem_limit_bytes=1024 * 1024),
        cost_estimate=cost(0, 4 * count * rows * width),
    )(*blocks)


def norm_into(xn_ref, x_ref, gain_ref, row, order_ref):
    wide = x_ref[...].astype(F32)
    inv = lax.rsqrt(jnp.mean(wide * wide, axis=-1, keepdims=True) + EPS)
    for k in range(32):
        at = pl.ds(pl.multiple_of(order_ref[k] * 128, 128), 128)
        part = x_ref[:, at].astype(F32) * inv * gain_ref[row : row + 1, at]
        xn_ref[:, k * 128 : (k + 1) * 128] = part.astype(BF16)


def attend(q, keys_ref, values_ref, resid, lengths_ref):
    seqs, heads = q.shape[0] // 128, q.shape[1] // HEAD
    position = lax.broadcasted_iota(jnp.int32, (heads * 128, 128), 1)
    made = []
    for m in range(seqs):
        rows = slice(m * 128, (m + 1) * 128)
        stacked = jnp.concatenate([q[rows, h * HEAD : (h + 1) * HEAD] for h in range(heads)], 0)
        scores = lax.dot_general(
            stacked, keys_ref[rows, :], (((1,), (1,)), ((), ())), preferred_element_type=F32
        )
        expd = jnp.where(position < lengths_ref[m], jnp.exp2(scores * LOG2E_SCALED), 0.0)
        probs = (expd * (1.0 / jnp.sum(expd, axis=-1, keepdims=True))).astype(BF16)
        context = dot(probs, values_ref[rows, :])
        made.append(jnp.concatenate([context[h * 128 : (h + 1) * 128] for h in range(heads)], 1))
    return (resid.astype(F32) + jnp.concatenate(made, 0)).astype(BF16)


def project_into(keys_ref, values_ref, xn_ref, kv, key_scale, value_scale):
    projected = dot(xn_ref[...], kv)
    keys_ref[...] = (projected[:, :HEAD] * key_scale).astype(BF16)
    values_ref[...] = (projected[:, HEAD:] * value_scale).astype(BF16)


def enter_kernel(order_ref, section_ref, source_ref, target_ref, gain_ref, x_ref, xn_ref):
    @pl.when(section_ref[0] == 2)
    def _():
        x_ref[...] = target_ref[...]

    @pl.when(section_ref[0] != 2)
    def _():
        x_ref[...] = source_ref[...]

    norm_into(xn_ref, x_ref, gain_ref, 0, order_ref)


def project_kernel(scale_ref, xn_ref, own_ref, other_ref, keys_ref, values_ref):
    kv = jnp.concatenate([own_ref[...], other_ref[...]], 0)
    project_into(keys_ref, values_ref, xn_ref, kv, scale_ref[1], scale_ref[2])


def part_kernel(lengths_ref, section_ref, scale_ref, xn_ref, own_ref, other_ref, k_ref, v_ref, x_ref, out_ref):
    half = own_ref.shape[0]
    acc = dot(xn_ref[:, :half], own_ref[...]) + dot(xn_ref[:, half:], other_ref[...])
    q = (acc * scale_ref[0]).astype(BF16)

    @pl.when(section_ref[0] != 2)
    def _():
        out_ref[...] = attend(q, k_ref, v_ref, x_ref[...], lengths_ref)

    @pl.when(section_ref[0] == 2)
    def _():
        out_ref[...] = q


def layer_part(xn, own, other, keys, values, x, at, width, lengths, section, scales, block):
    rows = xn.shape[0]
    depth = own.shape[0]
    whole = lambda a: pl.BlockSpec(a.shape, lambda j: (0, 0))
    return pl.pallas_call(
        part_kernel,
        grid=(width // block,),
        out_shape=jax.ShapeDtypeStruct((rows, width), BF16),
        in_specs=[
            SMEM,
            SMEM,
            SMEM,
            whole(xn),
            pl.BlockSpec((depth, block), lambda j: (0, j)),
            pl.BlockSpec((depth, block), lambda j: (0, j)),
            whole(keys),
            whole(values),
            pl.BlockSpec((rows, block), lambda j: (0, at // block + j)),
        ],
        out_specs=pl.BlockSpec((rows, block), lambda j: (0, j)),
        compiler_params=params(),
        cost_estimate=cost(4 * rows * depth * width, 4 * depth * width, rows * width),
    )(lengths, section, scales, xn, own, other, keys, values, x)


def stream_layer(parts, buf, sems, xn_ref, q_ref, k_ref, v_ref, x_ref, lengths_ref, scale, out_ref):
    half = buf.shape[1] // 2
    firsts = [0]
    for width in PARTS:
        firsts.append(firsts[-1] + width // BLOCK)
    blocks = firsts[-1]

    def pair(own, other, at, slot):
        columns = pl.ds(at, BLOCK)
        return (
            pltpu.make_async_copy(own.at[:, columns], buf.at[slot, pl.ds(0, half)], sems.at[slot, 0]),
            pltpu.make_async_copy(other.at[:, columns], buf.at[slot, pl.ds(half, half)], sems.at[slot, 1]),
        )

    def begin(b):
        slot = lax.rem(b, SLOTS)
        for i, (own, other) in enumerate(parts):

            @pl.when((b >= firsts[i]) & (b < firsts[i + 1]))
            def _():
                for copy in pair(own, other, pl.multiple_of((b - firsts[i]) * BLOCK, BLOCK), slot):
                    copy.start()

    def start():
        for b in range(SLOTS - 1):
            begin(jnp.int32(b))

    def run():
        q_ref[...] = jnp.zeros_like(q_ref)

        def emit(b):
            columns = pl.ds(pl.multiple_of(b * BLOCK, BLOCK), BLOCK)
            out_ref[:, columns] = attend(q_ref[...], k_ref, v_ref, x_ref[:, columns], lengths_ref)

        def step(b, carry):
            slot = lax.rem(b, SLOTS)
            for copy in pair(*parts[0], 0, slot):
                copy.wait()

            @pl.when(b + SLOTS - 1 < blocks)
            def _():
                begin(b + SLOTS - 1)

            acc = dot(xn_ref[...], buf[slot])
            emit(jnp.maximum(b - 1, 0))
            q_ref[...] = (acc * scale).astype(BF16)
            return carry

        lax.fori_loop(0, blocks, step, 0)
        emit(jnp.int32(blocks - 1))

    return start, run


def bring(pieces, out_ref, sems):
    at = 0
    copies = []
    for i, piece in enumerate(pieces):
        copies.append(pltpu.make_async_copy(piece, out_ref.at[:, pl.ds(at, piece.shape[1])], sems.at[i]))
        at += piece.shape[1]
    return copies


def encoder_kernel(*refs):
    n = len(PARTS)
    order_ref, section_ref, lengths_ref, scale_ref, gain_ref = refs[:5]
    pieces = refs[5 : 5 + n]
    flat = refs[5 + n : 5 + 3 * n]
    parts = [(flat[2 * i], flat[2 * i + 1]) for i in range(n)]
    kv_refs = refs[5 + 3 * n : 9 + 3 * n]
    out_ref, cross_ref = refs[9 + 3 * n : 11 + 3 * n]
    buf, sems, kv_buf, kv_sems, x_ref, x_sems, xn_ref, q_ref, k_ref, v_ref = refs[11 + 3 * n :]
    half = kv_buf.shape[1] // 2
    kv_at = pl.ds(PARTS[0], 2 * HEAD)

    @pl.when(section_ref[0] == 1)
    def _():
        arrive = bring(pieces, x_ref, x_sems)
        for copy in arrive:
            copy.start()
        kv_parts = [
            (parts[0][0].at[:, kv_at], parts[0][1].at[:, kv_at]),
            (kv_refs[0], kv_refs[1]),
            (kv_refs[2], kv_refs[3]),
        ]
        kv_copies = []
        for i, halves in enumerate(kv_parts):
            for c, ref in enumerate(halves):
                kv_copies.append(
                    pltpu.make_async_copy(ref, kv_buf.at[i, pl.ds(c * half, half)], kv_sems.at[i, c])
                )
        for copy in kv_copies[:2]:
            copy.start()
        start, run = stream_layer(
            parts, buf, sems, xn_ref, q_ref, k_ref, v_ref, x_ref, lengths_ref, scale_ref[0], out_ref
        )
        start()
        for copy in kv_copies[2:]:
            copy.start()
        for copy in arrive:
            copy.wait()
        norm_into(xn_ref, x_ref, gain_ref, 0, order_ref)
        for copy in kv_copies[:2]:
            copy.wait()
        project_into(k_ref, v_ref, xn_ref, kv_buf[0], scale_ref[1], scale_ref[2])
        run()
        for copy in kv_copies[2:]:
            copy.wait()
        for i in (1, 2):
            norm_into(xn_ref, out_ref, gain_ref, i, order_ref)
            at = (i - 1) * 2 * HEAD
            project_into(
                cross_ref.at[:, pl.ds(at, HEAD)],
                cross_ref.at[:, pl.ds(at + HEAD, HEAD)],
                xn_ref,
                kv_buf[i],
                scale_ref[3 * i + 1],
                scale_ref[3 * i + 2],
            )


def decoder_kernel(*refs):
    n = len(PARTS)
    order_ref, section_ref, lengths_ref, scale_ref, gain_ref, cross_ref, first_out, target = refs[:8]
    made = refs[8 : 8 + n]
    passed = refs[8 + n : 8 + 2 * n]
    flat = refs[8 + 2 * n : 8 + 4 * n]
    parts = [(flat[2 * i], flat[2 * i + 1]) for i in range(n)]
    out_ref = refs[8 + 4 * n]
    buf, sems, x_ref, x_sems, mid_ref, xn_ref, q_ref = refs[9 + 4 * n :]
    section = section_ref[0]
    blocks = sum(PARTS) // BLOCK
    cols = lambda i: cross_ref.at[:, pl.ds(i * HEAD, HEAD)]

    def fetch(pieces, into):
        copies = bring(pieces, into, x_sems)
        for copy in copies:
            copy.start()
        for copy in copies:
            copy.wait()

    def attend_all(resid_ref, into):
        def step(b, carry):
            columns = pl.ds(pl.multiple_of(b * BLOCK, BLOCK), BLOCK)
            into[:, columns] = attend(x_ref[:, columns], cols(0), cols(1), resid_ref[:, columns], lengths_ref)
            return carry

        lax.fori_loop(0, blocks, step, 0)

    @pl.when(section == 0)
    def _():
        fetch(made, out_ref)

    @pl.when(section == 1)
    def _():
        fetch([first_out], out_ref)

    @pl.when(section == 2)
    def _():
        fetch(made, x_ref)
        attend_all(target, out_ref)

    @pl.when(section == 3)
    def _():
        start, run = stream_layer(
            parts, buf, sems, xn_ref, q_ref, cols(2), cols(3), mid_ref, lengths_ref, scale_ref[0], out_ref
        )
        copies = bring(passed, x_ref, x_sems)
        for copy in copies:
            copy.start()
        start()
        for copy in copies:
            copy.wait()
        attend_all(target, mid_ref)
        norm_into(xn_ref, mid_ref, gain_ref, 0, order_ref)
        run()


def unit_direction(along):
    return (along * lax.rsqrt(jnp.sum(along * along) + EPS)).astype(BF16)


def spectral(weight, kv_part, start_rows, gamma):
    width = weight.shape[1]
    of_kv = dot(start_rows, kv_part)
    parts = jnp.concatenate([dot(start_rows[0:1], weight)[0], of_kv[1, :HEAD], of_kv[2, HEAD:]])
    along = total(parts.reshape(-1, 128)).reshape(-1)
    images = jnp.stack(
        [
            dot(weight, unit_direction(along[:width])),
            dot(kv_part[:, :HEAD], unit_direction(along[width : width + HEAD])),
            dot(kv_part[:, HEAD:], unit_direction(along[width + HEAD :])),
        ]
    )
    squares = jnp.sum(images * images, axis=1)
    totals = total(jnp.broadcast_to(squares[:, None], (3, 128)))[:, 0]
    sigmas = jnp.sqrt(totals + EPS)
    return gamma / sigmas, images / sigmas[:, None], along


def shards(weights, kv_weights, gammas, gains, starts, source, target, lengths):
    weight, kv_part, gamma, gain, start_rows = weights[0], kv_weights[0], gammas[0], gains[0], starts[0]
    width = weight.shape[1]
    section = lax.axis_index("section").astype(jnp.int32).reshape(1)
    micro, seqs, length, _ = source.shape
    rows = micro * seqs * length
    seq_lengths = lengths.reshape(-1)
    source2 = source.reshape(rows, width)
    target2 = target.reshape(rows, width)
    wide_gain = gain.astype(F32).reshape(1, width)
    row_shape = jax.ShapeDtypeStruct((rows, width), BF16)
    head_shape = jax.ShapeDtypeStruct((rows, HEAD), BF16)

    hop = lambda value, pairs: lax.ppermute(value, "section", pairs)
    order = row_order()
    scales, next_part, along = spectral(weight, kv_part, start_rows, gamma)

    x0, xn0 = pl.pallas_call(
        enter_kernel,
        out_shape=(row_shape, row_shape),
        in_specs=[SMEM, SMEM, VMEM, VMEM, VMEM],
        out_specs=(VMEM, VMEM),
        compiler_params=params(),
        cost_estimate=cost(8 * rows * width, 8 * rows * width),
    )(order, section, source2, target2, wide_gain)

    ends = [sum(PARTS[: i + 1]) for i in range(len(PARTS))]
    head_block = jnp.concatenate([weight[:, : ends[0]], kv_part], 1)
    tail_block = weight[:, ends[0] :]
    head_line = ring(head_block, first_move, True)
    tail_block, _ = lax.optimization_barrier((tail_block, along))
    tail_line = ring(tail_block, first_move, False)
    gathered = []
    for i in range(len(PARTS)):
        if i == 0:
            line = stack(head_line)
        else:
            line = stack([a[:, ends[i - 1] - ends[0] : ends[i] - ends[0]] for a in tail_line])
        if i == 1:
            line, scales = lax.optimization_barrier((line, scales))
        own = stack(ring(line, second_move, i % 2 == 0))
        gathered.append((own, send(own, CORE_SWAP)))
    kv_own, kv_other = (a[:, PARTS[0] :] for a in gathered[0])

    kv2_own = hop(kv_own, [(2, 1)])
    kv3_own = hop(kv_own, [(3, 1)])
    kv2_other = send(kv2_own, CORE_SWAP)
    kv3_other = send(kv3_own, CORE_SWAP)
    small = jnp.concatenate([gain.astype(F32), jnp.pad(scales, (0, 125))]).reshape(-1, 128)
    small2 = hop(small, [(2, 1)]).reshape(-1)
    small3 = hop(small, [(3, 1)]).reshape(-1)

    depth = gathered[0][0].shape[0]
    kv_block = pl.BlockSpec((depth, 2 * HEAD), lambda j: (0, PARTS[0] // (2 * HEAD)))
    whole = lambda shape: pl.BlockSpec(shape, lambda j: (0, 0))
    keys, values = pl.pallas_call(
        project_kernel,
        grid=(1,),
        out_shape=(head_shape, head_shape),
        in_specs=[SMEM, whole((rows, width)), kv_block, kv_block],
        out_specs=(whole((rows, HEAD)), whole((rows, HEAD))),
        compiler_params=params(),
        cost_estimate=cost(4 * rows * width * HEAD, 4 * width * HEAD),
    )(scales, xn0, *gathered[0])

    made, passed = [], []
    for i, (own, other) in enumerate(gathered):
        part = layer_part(
            xn0, own, other, keys, values, x0, ends[i] - PARTS[i], PARTS[i], seq_lengths, section, scales, BLOCK
        )
        made.append(part)
        passed.append(hop(part, [(0, 1), (2, 3)]))
    flat = [half for halves in gathered for half in halves]

    scratch = [
        pltpu.VMEM((SLOTS, 2 * depth, BLOCK), BF16),
        pltpu.SemaphoreType.DMA((SLOTS, 2)),
    ]
    n = len(PARTS)
    all_scales = jnp.concatenate([scales, small2[width : width + 3], small3[width : width + 3]])
    all_gains = jnp.concatenate([wide_gain, small2[None, :width], small3[None, :width]], 0)
    layer_cost = cost(2 * rows * width * width, 2 * width * width, rows * width)
    out1, cross = pl.pallas_call(
        encoder_kernel,
        out_shape=(row_shape, jax.ShapeDtypeStruct((rows, 4 * HEAD), BF16)),
        in_specs=[SMEM] * 4 + [VMEM] + [ANY] * (3 * n + 4),
        out_specs=(VMEM, VMEM),
        scratch_shapes=scratch
        + [
            pltpu.VMEM((3, 2 * depth, 2 * HEAD), BF16),
            pltpu.SemaphoreType.DMA((3, 2)),
            pltpu.VMEM((rows, width), BF16),
            pltpu.SemaphoreType.DMA((n,)),
            pltpu.VMEM((rows, width), BF16),
            pltpu.VMEM((rows, BLOCK), BF16),
            pltpu.VMEM((rows, HEAD), BF16),
            pltpu.VMEM((rows, HEAD), BF16),
        ],
        compiler_params=params(),
        cost_estimate=layer_cost,
    )(order, section, seq_lengths, all_scales, all_gains, *passed, *flat, kv2_own, kv2_other, kv3_own, kv3_other)
    cross = hop(cross, [(1, 2)]) + hop(cross, [(1, 3)])

    result = pl.pallas_call(
        decoder_kernel,
        out_shape=row_shape,
        in_specs=[SMEM] * 4 + [VMEM, VMEM, ANY, VMEM] + [ANY] * (4 * n),
        out_specs=VMEM,
        scratch_shapes=scratch
        + [
            pltpu.VMEM((rows, width), BF16),
            pltpu.SemaphoreType.DMA((n,)),
            pltpu.VMEM((rows, width), BF16),
            pltpu.VMEM((rows, width), BF16),
            pltpu.VMEM((rows, BLOCK), BF16),
        ],
        compiler_params=params(),
        cost_estimate=layer_cost,
    )(order, section, seq_lengths, scales, wide_gain, cross, out1, target2, *made, *passed, *flat)
    return result.reshape(1, micro, seqs, length, width), next_part[None]


def solution(mesh):
    in_specs = (
        P("section", "fsdp", None),
        P("section", "fsdp", None),
        P("section", None),
        P("section", None),
        P("section", None, "fsdp"),
        P(None, "fsdp", None, None),
        P(None, "fsdp", None, None),
        P(None, "fsdp"),
    )
    out_specs = (P("section", None, "fsdp", None, None), P("section", None, "fsdp"))
    return jax.shard_map(shards, mesh=mesh, in_specs=in_specs, out_specs=out_specs, check_vma=False)
```

```python
import functools
import math

import jax
import jax.numpy as jnp
from jax import lax
from jax.experimental import pallas as pl
from jax.experimental.pallas import tpu as pltpu
from jax.sharding import PartitionSpec as P

HEAD = 128
EPS = 1e-06
F32 = jnp.float32
BF16 = jnp.bfloat16
VMEM_LIMIT = 48 * 1024 * 1024
BLOCK = 512
ROUTE = (0, -1, 1, 2)
PARTS = (1024, 1024, 1024, 1024)
SLOTS = 3
LOG2E_SCALED = math.log2(math.e) / math.sqrt(HEAD)
ANY = pl.BlockSpec(memory_space=pl.ANY)
VMEM = pl.BlockSpec(memory_space=pltpu.VMEM)
SMEM = pl.BlockSpec(memory_space=pltpu.SMEM)


def dot(a, b):
    return jnp.dot(a, b, preferred_element_type=F32)


def moves(fn):
    pairs = []
    for index in range(32):
        x, z, core = index // 8, (index // 2) % 4, index % 2
        x2, z2, core2 = fn(x, z, core)
        pairs.append((index, (x2 % 4) * 8 + (z2 % 4) * 2 + core2))
    return pairs


def first_move(step):
    return moves(lambda x, z, c: (x, z + step, c) if c == 0 else (x + step, z, c))


def second_move(step):
    return moves(lambda x, z, c: (x + step, z, c) if c == 0 else (x, z + step, c))


CORE_SWAP = moves(lambda x, z, c: (x, z, 1 - c))
DOUBLING = (
    CORE_SWAP,
    moves(lambda x, z, c: (x, z ^ 1, c)),
    moves(lambda x, z, c: (x ^ 1, z, c)),
    moves(lambda x, z, c: (x, z ^ 2, c)),
    moves(lambda x, z, c: (x ^ 2, z, c)),
)


def send(value, pairs):
    return lax.ppermute(value, "fsdp", pairs)


def behind(value, *others):
    return lax.optimization_barrier((value, *others))[0]


def near(block, move):
    return [block, send(block, move(1)), send(block, move(-1))]


def ring(blocks, move, forward, *first):
    far = send(behind(blocks[1], *first), move(1)) if forward else send(behind(blocks[2], *first), move(-1))
    return blocks + [far]


def row_order():
    index = lax.axis_index("fsdp")
    x, z, core = index // 8, (index // 2) % 4, index % 2
    first = jnp.array(ROUTE, jnp.int32)
    line = jnp.tile(first, 4)
    plane = jnp.repeat(first, 4)

    def order(kind):
        zs = z + jnp.where(kind == 0, line, plane)
        xs = x + jnp.where(kind == 0, plane, line)
        return ((xs + 8) % 4) * 8 + ((zs + 8) % 4) * 2 + kind

    return jnp.concatenate([order(core), order(1 - core)]).astype(jnp.int32)


def total(value, blocks):
    for i, pairs in enumerate(DOUBLING):
        if i == 3:
            value = behind(value, *blocks)
        value = value + send(value, pairs)
    return value


def params():
    return pltpu.CompilerParams(vmem_limit_bytes=VMEM_LIMIT)


def cost(flops, size, exps=0):
    share = 64
    return pl.CostEstimate(flops=int(flops) // share, bytes_accessed=int(size) // share, transcendentals=int(exps) // share)


def stack_kernel(count, *refs):
    sources, out, sems = refs[:count], refs[count], refs[count + 1]
    rows = sources[0].shape[0]
    copies = [
        pltpu.make_async_copy(source, out.at[pl.ds(i * rows, rows)], sems.at[i])
        for i, source in enumerate(sources)
    ]
    for copy in copies:
        copy.start()
    for copy in copies:
        copy.wait()


def stack(blocks):
    count = len(blocks)
    rows, width = blocks[0].shape
    return pl.pallas_call(
        functools.partial(stack_kernel, count),
        out_shape=jax.ShapeDtypeStruct((count * rows, width), blocks[0].dtype),
        in_specs=[ANY] * count,
        out_specs=ANY,
        scratch_shapes=[pltpu.SemaphoreType.DMA((count,))],
        compiler_params=pltpu.CompilerParams(vmem_limit_bytes=1024 * 1024),
        cost_estimate=cost(0, 4 * count * rows * width),
    )(*blocks)


def norm_into(xn_ref, x_ref, gain_ref, row, order_ref):
    wide = x_ref[...].astype(F32)
    inv = lax.rsqrt(jnp.mean(wide * wide, axis=-1, keepdims=True) + EPS)
    for k in range(32):
        at = pl.ds(pl.multiple_of(order_ref[k] * 128, 128), 128)
        part = x_ref[:, at].astype(F32) * inv * gain_ref[row : row + 1, at]
        xn_ref[:, k * 128 : (k + 1) * 128] = part.astype(BF16)


def attend(q, keys_ref, values_ref, resid, lengths_ref, key_scale, value_scale):
    seqs, heads = q.shape[0] // 128, q.shape[1] // HEAD
    position = lax.broadcasted_iota(jnp.int32, (heads * 128, 128), 1)
    made = []
    for m in range(seqs):
        rows = slice(m * 128, (m + 1) * 128)
        stacked = jnp.concatenate([q[rows, h * HEAD : (h + 1) * HEAD] for h in range(heads)], 0)
        scores = lax.dot_general(
            stacked, keys_ref[rows, :], (((1,), (1,)), ((), ())), preferred_element_type=F32
        )
        expd = jnp.where(position < lengths_ref[m], jnp.exp2(scores * (key_scale * LOG2E_SCALED)), 0.0)
        probs = (expd * (1.0 / jnp.sum(expd, axis=-1, keepdims=True))).astype(BF16)
        context = dot(probs, values_ref[rows, :]) * value_scale
        made.append(jnp.concatenate([context[h * 128 : (h + 1) * 128] for h in range(heads)], 1))
    return (resid.astype(F32) + jnp.concatenate(made, 0)).astype(BF16)


def project_into(keys_ref, values_ref, xn_ref, kv):
    projected = dot(xn_ref[...], kv).astype(BF16)
    keys_ref[...] = projected[:, :HEAD]
    values_ref[...] = projected[:, HEAD:]


def enter_kernel(order_ref, section_ref, source_ref, target_ref, gain_ref, x_ref, xn_ref):
    @pl.when(section_ref[0] == 2)
    def _():
        x_ref[...] = target_ref[...]

    @pl.when(section_ref[0] != 2)
    def _():
        x_ref[...] = source_ref[...]

    norm_into(xn_ref, x_ref, gain_ref, 0, order_ref)


def project_kernel(xn_ref, own_ref, other_ref, keys_ref, values_ref):
    project_into(keys_ref, values_ref, xn_ref, jnp.concatenate([own_ref[...], other_ref[...]], 0))


def part_kernel(lengths_ref, section_ref, scale_ref, xn_ref, own_ref, other_ref, k_ref, v_ref, x_ref, out_ref):
    half = own_ref.shape[0]
    acc = dot(xn_ref[:, :half], own_ref[...]) + dot(xn_ref[:, half:], other_ref[...])
    q = (acc * scale_ref[0]).astype(BF16)

    @pl.when(section_ref[0] != 2)
    def _():
        out_ref[...] = attend(q, k_ref, v_ref, x_ref[...], lengths_ref, scale_ref[1], scale_ref[2])

    @pl.when(section_ref[0] == 2)
    def _():
        out_ref[...] = q


def layer_part(xn, own, other, keys, values, x, at, width, lengths, section, scales, block):
    rows = xn.shape[0]
    depth = own.shape[0]
    whole = lambda a: pl.BlockSpec(a.shape, lambda j: (0, 0))
    return pl.pallas_call(
        part_kernel,
        grid=(width // block,),
        out_shape=jax.ShapeDtypeStruct((rows, width), BF16),
        in_specs=[
            SMEM,
            SMEM,
            SMEM,
            whole(xn),
            pl.BlockSpec((depth, block), lambda j: (0, j)),
            pl.BlockSpec((depth, block), lambda j: (0, j)),
            whole(keys),
            whole(values),
            pl.BlockSpec((rows, block), lambda j: (0, at // block + j)),
        ],
        out_specs=pl.BlockSpec((rows, block), lambda j: (0, j)),
        compiler_params=params(),
        cost_estimate=cost(4 * rows * depth * width, 4 * depth * width, rows * width),
    )(lengths, section, scales, xn, own, other, keys, values, x)


def stream_layer(parts, buf, sems, xn_ref, q_ref, k_ref, v_ref, x_ref, lengths_ref, scale_ref, out_ref):
    half = buf.shape[1] // 2
    firsts = [0]
    for width in PARTS:
        firsts.append(firsts[-1] + width // BLOCK)
    blocks = firsts[-1]

    def pair(own, other, at, slot):
        columns = pl.ds(at, BLOCK)
        return (
            pltpu.make_async_copy(own.at[:, columns], buf.at[slot, pl.ds(0, half)], sems.at[slot, 0]),
            pltpu.make_async_copy(other.at[:, columns], buf.at[slot, pl.ds(half, half)], sems.at[slot, 1]),
        )

    def begin(b):
        slot = lax.rem(b, SLOTS)
        for i, (own, other) in enumerate(parts):

            @pl.when((b >= firsts[i]) & (b < firsts[i + 1]))
            def _():
                for copy in pair(own, other, pl.multiple_of((b - firsts[i]) * BLOCK, BLOCK), slot):
                    copy.start()

    def start():
        for b in range(SLOTS - 1):
            begin(jnp.int32(b))

    def run():
        q_ref[...] = jnp.zeros_like(q_ref)

        def emit(b):
            columns = pl.ds(pl.multiple_of(b * BLOCK, BLOCK), BLOCK)
            out_ref[:, columns] = attend(
                q_ref[...], k_ref, v_ref, x_ref[:, columns], lengths_ref, scale_ref[1], scale_ref[2]
            )

        def step(b, carry):
            slot = lax.rem(b, SLOTS)
            for copy in pair(*parts[0], 0, slot):
                copy.wait()

            @pl.when(b + SLOTS - 1 < blocks)
            def _():
                begin(b + SLOTS - 1)

            acc = dot(xn_ref[...], buf[slot])
            emit(jnp.maximum(b - 1, 0))
            q_ref[...] = (acc * scale_ref[0]).astype(BF16)
            return carry

        lax.fori_loop(0, blocks, step, 0)
        emit(jnp.int32(blocks - 1))

    return start, run


def bring(pieces, out_ref, sems):
    at = 0
    copies = []
    for i, piece in enumerate(pieces):
        copies.append(pltpu.make_async_copy(piece, out_ref.at[:, pl.ds(at, piece.shape[1])], sems.at[i]))
        at += piece.shape[1]
    return copies


def encoder_kernel(*refs):
    n = len(PARTS)
    order_ref, section_ref, lengths_ref, scale_ref, gain_ref = refs[:5]
    pieces = refs[5 : 5 + n]
    flat = refs[5 + n : 5 + 3 * n]
    parts = [(flat[2 * i], flat[2 * i + 1]) for i in range(n)]
    out_ref, cross_ref = refs[5 + 3 * n : 7 + 3 * n]
    buf, sems, kv_buf, kv_sems, x_ref, x_sems, xn_ref, q_ref, k_ref, v_ref = refs[7 + 3 * n :]
    half = kv_buf.shape[1] // 2

    @pl.when(section_ref[0] == 1)
    def _():
        arrive = bring(pieces, x_ref, x_sems)
        for copy in arrive:
            copy.start()
        kv_copies = []
        for i, (part, at) in enumerate(((0, PARTS[0]), (1, PARTS[1]), (1, PARTS[1] + 2 * HEAD))):
            for c, ref in enumerate(parts[part]):
                kv_copies.append(
                    pltpu.make_async_copy(
                        ref.at[:, pl.ds(at, 2 * HEAD)], kv_buf.at[i, pl.ds(c * half, half)], kv_sems.at[i, c]
                    )
                )
        for copy in kv_copies[:2]:
            copy.start()
        start, run = stream_layer(
            parts, buf, sems, xn_ref, q_ref, k_ref, v_ref, x_ref, lengths_ref, scale_ref, out_ref
        )
        start()
        for copy in kv_copies[2:]:
            copy.start()
        for copy in arrive:
            copy.wait()
        norm_into(xn_ref, x_ref, gain_ref, 0, order_ref)
        for copy in kv_copies[:2]:
            copy.wait()
        project_into(k_ref, v_ref, xn_ref, kv_buf[0])
        run()
        for copy in kv_copies[2:]:
            copy.wait()
        for i in (1, 2):
            norm_into(xn_ref, out_ref, gain_ref, i, order_ref)
            at = (i - 1) * 2 * HEAD
            project_into(
                cross_ref.at[:, pl.ds(at, HEAD)],
                cross_ref.at[:, pl.ds(at + HEAD, HEAD)],
                xn_ref,
                kv_buf[i],
            )


def decoder_kernel(*refs):
    n = len(PARTS)
    order_ref, section_ref, lengths_ref, scale_ref, gain_ref, cross_ref, first_out, target = refs[:8]
    made = refs[8 : 8 + n]
    passed = refs[8 + n : 8 + 2 * n]
    flat = refs[8 + 2 * n : 8 + 4 * n]
    parts = [(flat[2 * i], flat[2 * i + 1]) for i in range(n)]
    out_ref = refs[8 + 4 * n]
    buf, sems, x_ref, x_sems, mid_ref, xn_ref, q_ref = refs[9 + 4 * n :]
    section = section_ref[0]
    blocks = sum(PARTS) // BLOCK
    cols = lambda i: cross_ref.at[:, pl.ds(i * HEAD, HEAD)]

    def fetch(pieces, into):
        copies = bring(pieces, into, x_sems)
        for copy in copies:
            copy.start()
        for copy in copies:
            copy.wait()

    def attend_all(resid_ref, into):
        def step(b, carry):
            columns = pl.ds(pl.multiple_of(b * BLOCK, BLOCK), BLOCK)
            into[:, columns] = attend(
                x_ref[:, columns], cols(0), cols(1), resid_ref[:, columns], lengths_ref, scale_ref[4], scale_ref[5]
            )
            return carry

        lax.fori_loop(0, blocks, step, 0)

    @pl.when(section == 0)
    def _():
        fetch(made, out_ref)

    @pl.when(section == 1)
    def _():
        fetch([first_out], out_ref)

    @pl.when(section == 2)
    def _():
        fetch(made, x_ref)
        attend_all(target, out_ref)

    @pl.when(section == 3)
    def _():
        start, run = stream_layer(
            parts, buf, sems, xn_ref, q_ref, cols(2), cols(3), mid_ref, lengths_ref, scale_ref, out_ref
        )
        copies = bring(passed, x_ref, x_sems)
        for copy in copies:
            copy.start()
        start()
        for copy in copies:
            copy.wait()
        attend_all(target, mid_ref)
        norm_into(xn_ref, mid_ref, gain_ref, 0, order_ref)
        run()


def unit_direction(along):
    return (along * lax.rsqrt(jnp.sum(along * along) + EPS)).astype(BF16)


def spectral_along(weight, kv_part, start_rows, block):
    of_kv = dot(start_rows, kv_part)
    parts = jnp.concatenate([dot(start_rows[0:1], weight)[0], of_kv[1, :HEAD], of_kv[2, HEAD:]])
    return total(parts.reshape(-1, 128), block).reshape(-1)


def spectral_scales(weight, kv_part, along, gamma, block):
    width = weight.shape[1]
    images = jnp.stack(
        [
            dot(weight, unit_direction(along[:width])),
            dot(kv_part[:, :HEAD], unit_direction(along[width : width + HEAD])),
            dot(kv_part[:, HEAD:], unit_direction(along[width + HEAD :])),
        ]
    )
    squares = jnp.sum(images * images, axis=1)
    totals = total(jnp.broadcast_to(squares[:, None], (3, 128)), block)[:, 0]
    sigmas = jnp.sqrt(totals + EPS)
    return gamma / sigmas, images / sigmas[:, None]


def shards(weights, kv_weights, gammas, gains, starts, source, target, lengths):
    weight, kv_part, gamma, gain, start_rows = weights[0], kv_weights[0], gammas[0], gains[0], starts[0]
    width = weight.shape[1]
    section = lax.axis_index("section").astype(jnp.int32).reshape(1)
    micro, seqs, length, _ = source.shape
    rows = micro * seqs * length
    seq_lengths = lengths.reshape(-1)
    source2 = source.reshape(rows, width)
    target2 = target.reshape(rows, width)
    wide_gain = gain.astype(F32).reshape(1, width)
    row_shape = jax.ShapeDtypeStruct((rows, width), BF16)
    head_shape = jax.ShapeDtypeStruct((rows, HEAD), BF16)

    hop = lambda value, pairs: lax.ppermute(value, "section", pairs)
    order = row_order()

    ends = [sum(PARTS[: i + 1]) for i in range(len(PARTS))]
    head_block = jnp.concatenate([weight[:, : ends[0]], kv_part], 1)
    head_line = ring(near(head_block, first_move), first_move, True)
    extra = jnp.concatenate([kv_part, gain.reshape(-1, 2 * HEAD)], 0)
    extra2 = hop(extra, [(2, 1)])
    extra3 = hop(extra, [(3, 1)])
    local = kv_part.shape[0]
    tail_block = jnp.concatenate(
        [weight[:, ends[0] : ends[1]], extra2[:local], extra3[:local], weight[:, ends[1] :]], 1
    )
    tail_line = ring(near(behind(tail_block, head_line[1], head_line[2]), first_move), first_move, False)

    def line_of(i):
        if i == 0:
            return stack(head_line)
        low, high = ends[i - 1] - ends[0], ends[i] - ends[0] + 4 * HEAD
        return stack([a[:, (low if i == 1 else low + 4 * HEAD) : high] for a in tail_line])

    x0, xn0 = pl.pallas_call(
        enter_kernel,
        out_shape=(row_shape, row_shape),
        in_specs=[SMEM, SMEM, VMEM, VMEM, VMEM],
        out_specs=(VMEM, VMEM),
        compiler_params=params(),
        cost_estimate=cost(8 * rows * width, 8 * rows * width),
    )(order, section, source2, target2, wide_gain)

    gathered, made, passed = [], [], []

    def first_part(i):
        own, other = gathered[i]
        part = layer_part(
            xn0, own, other, keys, values, x0, ends[i] - PARTS[i], PARTS[i], seq_lengths, section, scales, BLOCK
        )
        made.append(part)
        passed.append(hop(part, [(0, 1), (2, 3)]))

    def finish(i, blocks, *first, late=()):
        blocks = ring(blocks, second_move, i % 2 == 0, *first)
        own = stack(blocks[:3] + [behind(blocks[3], *late)])
        gathered.append((own, send(own, CORE_SWAP)))
        return blocks

    line = line_of(0)
    blocks0 = near(line, second_move)
    along = spectral_along(weight, kv_part, behind(start_rows, line), blocks0[1:2])
    blocks0 = finish(0, blocks0, along)
    blocks1 = near(line_of(1), second_move)
    scales, next_part = spectral_scales(weight, kv_part, behind(along, blocks0[2]), gamma, (blocks0[3], blocks1[1]))
    lines = {2: line_of(2)}
    finish(1, blocks1, scales, gathered[0][0], late=(lines[2],))

    depth = gathered[0][0].shape[0]
    kv_block = pl.BlockSpec((depth, 2 * HEAD), lambda j: (0, PARTS[0] // (2 * HEAD)))
    whole = lambda shape: pl.BlockSpec(shape, lambda j: (0, 0))
    keys, values = pl.pallas_call(
        project_kernel,
        grid=(1,),
        out_shape=(head_shape, head_shape),
        in_specs=[whole((rows, width)), kv_block, kv_block],
        out_specs=(whole((rows, HEAD)), whole((rows, HEAD))),
        compiler_params=params(),
        cost_estimate=cost(4 * rows * width * HEAD, 4 * width * HEAD),
    )(xn0, *gathered[0])
    scales2 = hop(jnp.broadcast_to(scales[:, None], (3, 128)), [(2, 3)])[:, 0]
    for i in range(2, len(PARTS)):
        blocks = near(behind(lines[i], gathered[i - 2][0]), second_move)
        if i + 1 < len(PARTS):
            lines[i + 1] = line_of(i + 1)
        first_part(i - 2)
        finish(i, blocks, made[-1], scales2, late=(lines[i + 1],) if i + 1 in lines else ())
    for i in range(len(made), len(PARTS)):
        first_part(i)
    flat = [half for halves in gathered for half in halves]

    scratch = [
        pltpu.VMEM((SLOTS, 2 * depth, BLOCK), BF16),
        pltpu.SemaphoreType.DMA((SLOTS, 2)),
    ]
    n = len(PARTS)
    all_gains = jnp.stack([gain, extra2[local:].reshape(-1), extra3[local:].reshape(-1)]).astype(F32)
    all_scales = jnp.concatenate([scales, jnp.where(section == 3, scales2, scales)])
    layer_cost = cost(2 * rows * width * width, 2 * width * width, rows * width)
    out1, cross = pl.pallas_call(
        encoder_kernel,
        out_shape=(row_shape, jax.ShapeDtypeStruct((rows, 4 * HEAD), BF16)),
        in_specs=[SMEM] * 4 + [VMEM] + [ANY] * (3 * n),
        out_specs=(VMEM, VMEM),
        scratch_shapes=scratch
        + [
            pltpu.VMEM((3, 2 * depth, 2 * HEAD), BF16),
            pltpu.SemaphoreType.DMA((3, 2)),
            pltpu.VMEM((rows, width), BF16),
            pltpu.SemaphoreType.DMA((n,)),
            pltpu.VMEM((rows, width), BF16),
            pltpu.VMEM((rows, BLOCK), BF16),
            pltpu.VMEM((rows, HEAD), BF16),
            pltpu.VMEM((rows, HEAD), BF16),
        ],
        compiler_params=params(),
        cost_estimate=layer_cost,
    )(order, section, seq_lengths, scales, all_gains, *passed, *flat)
    cross = hop(cross, [(1, 2)]) + hop(cross, [(1, 3)])

    result = pl.pallas_call(
        decoder_kernel,
        out_shape=row_shape,
        in_specs=[SMEM] * 4 + [VMEM, VMEM, ANY, VMEM] + [ANY] * (4 * n),
        out_specs=VMEM,
        scratch_shapes=scratch
        + [
            pltpu.VMEM((rows, width), BF16),
            pltpu.SemaphoreType.DMA((n,)),
            pltpu.VMEM((rows, width), BF16),
            pltpu.VMEM((rows, width), BF16),
            pltpu.VMEM((rows, BLOCK), BF16),
        ],
        compiler_params=params(),
        cost_estimate=layer_cost,
    )(order, section, seq_lengths, all_scales, wide_gain, cross, out1, target2, *made, *passed, *flat)
    return result.reshape(1, micro, seqs, length, width), next_part[None]


def solution(mesh):
    in_specs = (
        P("section", "fsdp", None),
        P("section", "fsdp", None),
        P("section", None),
        P("section", None),
        P("section", None, "fsdp"),
        P(None, "fsdp", None, None),
        P(None, "fsdp", None, None),
        P(None, "fsdp"),
    )
    out_specs = (P("section", None, "fsdp", None, None), P("section", None, "fsdp"))
    return jax.shard_map(shards, mesh=mesh, in_specs=in_specs, out_specs=out_specs, check_vma=False)
```

```python
import functools
import math

import jax
import jax.numpy as jnp
from jax import lax
from jax.experimental import pallas as pl
from jax.experimental.pallas import tpu as pltpu
from jax.sharding import PartitionSpec as P

HEAD = 128
EPS = 1e-06
F32 = jnp.float32
BF16 = jnp.bfloat16
VMEM_LIMIT = 48 * 1024 * 1024
BLOCK = 512
PIECE = 1024
SLOTS = 3
LOG2E_SCALED = math.log2(math.e) / math.sqrt(HEAD)
ANY = pl.BlockSpec(memory_space=pl.ANY)
VMEM = pl.BlockSpec(memory_space=pltpu.VMEM)
SMEM = pl.BlockSpec(memory_space=pltpu.SMEM)


def dot(a, b):
    return jnp.dot(a, b, preferred_element_type=F32)


def moves(fn):
    pairs = []
    for index in range(32):
        x, z, core = index // 8, (index // 2) % 4, index % 2
        x2, z2, core2 = fn(x, z, core)
        pairs.append((index, (x2 % 4) * 8 + (z2 % 4) * 2 + core2))
    return pairs


CORE_SWAP = moves(lambda x, z, c: (x, z, 1 - c))
DOUBLING = (
    CORE_SWAP,
    moves(lambda x, z, c: (x, z ^ 1, c)),
    moves(lambda x, z, c: (x ^ 1, z, c)),
    moves(lambda x, z, c: (x, z ^ 2, c)),
    moves(lambda x, z, c: (x ^ 2, z, c)),
)


def send(value, pairs):
    return lax.ppermute(value, "fsdp", pairs)


def total(value):
    for pairs in DOUBLING:
        value = value + send(value, pairs)
    return value


def params():
    return pltpu.CompilerParams(vmem_limit_bytes=VMEM_LIMIT)


def cost(flops, size, exps=0):
    share = 64
    return pl.CostEstimate(flops=int(flops) // share, bytes_accessed=int(size) // share, transcendentals=int(exps) // share)


def norm_into(xn_ref, x_ref, gain_ref, row):
    wide = x_ref[...].astype(F32)
    inv = lax.rsqrt(jnp.mean(wide * wide, axis=-1, keepdims=True) + EPS)
    xn_ref[...] = (wide * inv * gain_ref[row : row + 1, :]).astype(BF16)


def attend(q, keys_ref, values_ref, resid, lengths_ref, key_scale, value_scale):
    seqs, heads = q.shape[0] // 128, q.shape[1] // HEAD
    position = lax.broadcasted_iota(jnp.int32, (heads * 128, 128), 1)
    made = []
    for m in range(seqs):
        rows = slice(m * 128, (m + 1) * 128)
        stacked = jnp.concatenate([q[rows, h * HEAD : (h + 1) * HEAD] for h in range(heads)], 0)
        scores = lax.dot_general(
            stacked, keys_ref[rows, :], (((1,), (1,)), ((), ())), preferred_element_type=F32
        )
        expd = jnp.where(position < lengths_ref[m], jnp.exp2(scores * (key_scale * LOG2E_SCALED)), 0.0)
        probs = (expd * (1.0 / jnp.sum(expd, axis=-1, keepdims=True))).astype(BF16)
        context = dot(probs, values_ref[rows, :]) * value_scale
        made.append(jnp.concatenate([context[h * 128 : (h + 1) * 128] for h in range(heads)], 1))
    return (resid.astype(F32) + jnp.concatenate(made, 0)).astype(BF16)


def project_into(keys_ref, values_ref, xn, kv):
    projected = dot(xn, kv).astype(BF16)
    keys_ref[...] = projected[:, :HEAD]
    values_ref[...] = projected[:, HEAD:]


def enter_kernel(section_ref, source_ref, target_ref, gain_ref, x_ref, xn_ref):
    @pl.when(section_ref[0] == 2)
    def _():
        x_ref[...] = target_ref[...]

    @pl.when(section_ref[0] != 2)
    def _():
        x_ref[...] = source_ref[...]

    norm_into(xn_ref, x_ref, gain_ref, 0)


def project_kernel(xn_ref, kv_ref, keys_ref, values_ref):
    project_into(keys_ref, values_ref, xn_ref[...], kv_ref[...])


def part_kernel(lengths_ref, section_ref, scale_ref, xn_ref, w_ref, k_ref, v_ref, x_ref, out_ref):
    q = (dot(xn_ref[...], w_ref[...]) * scale_ref[0]).astype(BF16)

    @pl.when(section_ref[0] != 2)
    def _():
        out_ref[...] = attend(q, k_ref, v_ref, x_ref[...], lengths_ref, scale_ref[1], scale_ref[2])

    @pl.when(section_ref[0] == 2)
    def _():
        out_ref[...] = q


def layer_part(xn, full, keys, values, x, at, lengths, section, scales):
    rows, width = xn.shape
    first = at // BLOCK
    whole = lambda a: pl.BlockSpec(a.shape, lambda j: (0, 0))
    return pl.pallas_call(
        part_kernel,
        grid=(PIECE // BLOCK,),
        out_shape=jax.ShapeDtypeStruct((rows, PIECE), BF16),
        in_specs=[
            SMEM,
            SMEM,
            SMEM,
            whole(xn),
            pl.BlockSpec((width, BLOCK), lambda j: (0, first + j)),
            whole(keys),
            whole(values),
            pl.BlockSpec((rows, BLOCK), lambda j: (0, first + j)),
        ],
        out_specs=pl.BlockSpec((rows, BLOCK), lambda j: (0, j)),
        compiler_params=params(),
        cost_estimate=cost(2 * rows * width * PIECE, 2 * width * PIECE, rows * PIECE),
    )(lengths, section, scales, xn, full, keys, values, x)


def stream_layer(full, buf, sems, xn_ref, q_ref, k_ref, v_ref, x_ref, lengths_ref, scale_ref, out_ref):
    blocks = x_ref.shape[1] // BLOCK

    def block(b):
        slot = lax.rem(b, SLOTS)
        at = pl.ds(pl.multiple_of(b * BLOCK, BLOCK), BLOCK)
        return pltpu.make_async_copy(full.at[:, at], buf.at[slot], sems.at[slot])

    def start():
        for b in range(SLOTS - 1):
            block(jnp.int32(b)).start()

    def run():
        q_ref[...] = jnp.zeros_like(q_ref)

        def emit(b):
            columns = pl.ds(pl.multiple_of(b * BLOCK, BLOCK), BLOCK)
            out_ref[:, columns] = attend(
                q_ref[...], k_ref, v_ref, x_ref[:, columns], lengths_ref, scale_ref[1], scale_ref[2]
            )

        def step(b, carry):
            slot = lax.rem(b, SLOTS)
            block(b).wait()

            @pl.when(b + SLOTS - 1 < blocks)
            def _():
                block(b + SLOTS - 1).start()

            acc = dot(xn_ref[...], buf[slot])
            emit(jnp.maximum(b - 1, 0))
            q_ref[...] = (acc * scale_ref[0]).astype(BF16)
            return carry

        lax.fori_loop(0, blocks, step, 0)
        emit(jnp.int32(blocks - 1))

    return start, run


def bring(pieces, out_ref, sems):
    at = 0
    copies = []
    for i, piece in enumerate(pieces):
        copies.append(pltpu.make_async_copy(piece, out_ref.at[:, pl.ds(at, piece.shape[1])], sems.at[i]))
        at += piece.shape[1]
    return copies


def encoder_kernel(count, *refs):
    section_ref, lengths_ref, scale_ref, gain_ref, full = refs[:5]
    pieces = refs[5 : 5 + count]
    out_ref, cross_ref = refs[5 + count : 7 + count]
    buf, sems, xn_ref, q_ref, x_ref, x_sems, kv_buf, kv_sems, k_ref, v_ref = refs[7 + count :]
    width = x_ref.shape[1]

    @pl.when(section_ref[0] == 1)
    def _():
        arrive = bring(pieces, x_ref, x_sems)
        for copy in arrive:
            copy.start()
        kv_copies = [
            pltpu.make_async_copy(
                full.at[:, pl.ds(width + i * 2 * HEAD, 2 * HEAD)], kv_buf.at[i], kv_sems.at[i]
            )
            for i in range(3)
        ]
        for copy in kv_copies[:1]:
            copy.start()
        start, run = stream_layer(
            full, buf, sems, xn_ref, q_ref, k_ref, v_ref, x_ref, lengths_ref, scale_ref, out_ref
        )
        start()
        for copy in kv_copies[1:]:
            copy.start()
        for copy in arrive:
            copy.wait()
        norm_into(xn_ref, x_ref, gain_ref, 0)
        for copy in kv_copies[:1]:
            copy.wait()
        project_into(k_ref, v_ref, xn_ref[...], kv_buf[0])
        run()
        for copy in kv_copies[1:]:
            copy.wait()
        for i in (1, 2):
            norm_into(xn_ref, out_ref, gain_ref, i)
            at = (i - 1) * 2 * HEAD
            project_into(
                cross_ref.at[:, pl.ds(at, HEAD)],
                cross_ref.at[:, pl.ds(at + HEAD, HEAD)],
                xn_ref[...],
                kv_buf[i],
            )


def decoder_kernel(count, *refs):
    section_ref, lengths_ref, scale_ref, gain_ref, full, cross_ref, first_out, target = refs[:8]
    made, passed = refs[8 : 8 + count], refs[8 + count : 8 + 2 * count]
    out_ref = refs[8 + 2 * count]
    buf, sems, xn_ref, q_ref, x_ref, x_sems, mid_ref = refs[9 + 2 * count :]
    section = section_ref[0]
    blocks = x_ref.shape[1] // BLOCK
    cols = lambda i: cross_ref.at[:, pl.ds(i * HEAD, HEAD)]

    def fetch(pieces, into):
        copies = bring(pieces, into, x_sems)
        for copy in copies:
            copy.start()
        for copy in copies:
            copy.wait()

    def attend_all(resid_ref, into):
        def step(b, carry):
            columns = pl.ds(pl.multiple_of(b * BLOCK, BLOCK), BLOCK)
            into[:, columns] = attend(
                x_ref[:, columns], cols(0), cols(1), resid_ref[:, columns], lengths_ref, scale_ref[4], scale_ref[5]
            )
            return carry

        lax.fori_loop(0, blocks, step, 0)

    @pl.when(section == 0)
    def _():
        fetch(made, out_ref)

    @pl.when(section == 1)
    def _():
        fetch([first_out], out_ref)

    @pl.when(section == 2)
    def _():
        fetch(made, x_ref)
        attend_all(target, out_ref)

    @pl.when(section == 3)
    def _():
        start, run = stream_layer(
            full, buf, sems, xn_ref, q_ref, cols(2), cols(3), mid_ref, lengths_ref, scale_ref, out_ref
        )
        copies = bring(passed, x_ref, x_sems)
        for copy in copies:
            copy.start()
        start()
        for copy in copies:
            copy.wait()
        attend_all(target, mid_ref)
        norm_into(xn_ref, mid_ref, gain_ref, 0)
        run()


def unit_direction(along):
    return (along * lax.rsqrt(jnp.sum(along * along) + EPS)).astype(BF16)


def spectral_along(weight, kv_part, start_rows):
    of_kv = dot(start_rows, kv_part)
    parts = jnp.concatenate([dot(start_rows[0:1], weight)[0], of_kv[1, :HEAD], of_kv[2, HEAD:]])
    return total(parts.reshape(-1, 128))


def spectral_images(weight, kv_part, along):
    width = weight.shape[1]
    return jnp.stack(
        [
            dot(weight, unit_direction(along[:width])),
            dot(kv_part[:, :HEAD], unit_direction(along[width : width + HEAD])),
            dot(kv_part[:, HEAD:], unit_direction(along[width + HEAD :])),
        ]
    )


def shards(weights, kv_weights, gammas, gains, starts, source, target, lengths):
    weight, kv_part, gamma, gain, start_rows = weights[0], kv_weights[0], gammas[0], gains[0], starts[0]
    width = weight.shape[1]
    section = lax.axis_index("section").astype(jnp.int32).reshape(1)
    micro, seqs, length, _ = source.shape
    rows = micro * seqs * length
    seq_lengths = lengths.reshape(-1)
    source2 = source.reshape(rows, width)
    target2 = target.reshape(rows, width)
    wide_gain = gain.astype(F32).reshape(1, width)
    row_shape = jax.ShapeDtypeStruct((rows, width), BF16)
    head_shape = jax.ShapeDtypeStruct((rows, HEAD), BF16)

    hop = lambda value, pairs: lax.ppermute(value, "section", pairs)

    extra = jnp.concatenate([kv_part, gain.reshape(-1, 2 * HEAD)], 0)
    extra2 = hop(extra, [(2, 1)])
    extra3 = hop(extra, [(3, 1)])
    local = kv_part.shape[0]

    full = jnp.concatenate([weight, kv_part, extra2[:local], extra3[:local]], 1)
    full = lax.all_gather(full, "fsdp", axis=0, tiled=True)

    along = spectral_along(weight, kv_part, start_rows).reshape(-1)
    images = spectral_images(weight, kv_part, along)
    squares = jnp.broadcast_to(jnp.sum(images * images, axis=1)[:, None], (3, 128))
    sigmas = jnp.sqrt(total(squares)[:, 0] + EPS)
    scales, next_part = gamma / sigmas, images / sigmas[:, None]
    scales2 = hop(jnp.broadcast_to(scales[:, None], (3, 128)), [(2, 3)])[:, 0]

    x0, xn0 = pl.pallas_call(
        enter_kernel,
        out_shape=(row_shape, row_shape),
        in_specs=[SMEM, VMEM, VMEM, VMEM],
        out_specs=(VMEM, VMEM),
        compiler_params=params(),
        cost_estimate=cost(8 * rows * width, 8 * rows * width),
    )(section, source2, target2, wide_gain)

    kv_block = pl.BlockSpec((width, 2 * HEAD), lambda j: (0, width // (2 * HEAD)))
    whole = lambda shape: pl.BlockSpec(shape, lambda j: (0, 0))
    keys, values = pl.pallas_call(
        project_kernel,
        grid=(1,),
        out_shape=(head_shape, head_shape),
        in_specs=[whole((rows, width)), kv_block],
        out_specs=(whole((rows, HEAD)), whole((rows, HEAD))),
        compiler_params=params(),
        cost_estimate=cost(4 * rows * width * HEAD, 4 * width * HEAD),
    )(xn0, full)

    made, passed = [], []
    for at in range(0, width, PIECE):
        made.append(layer_part(xn0, full, keys, values, x0, at, seq_lengths, section, scales))
        passed.append(hop(made[-1], [(0, 1), (2, 3)]))

    scratch = [
        pltpu.VMEM((SLOTS, width, BLOCK), BF16),
        pltpu.SemaphoreType.DMA((SLOTS,)),
        pltpu.VMEM((rows, width), BF16),
        pltpu.VMEM((rows, BLOCK), BF16),
        pltpu.VMEM((rows, width), BF16),
        pltpu.SemaphoreType.DMA((len(made),)),
    ]
    n = len(made)
    all_gains = jnp.stack([gain, extra2[local:].reshape(-1), extra3[local:].reshape(-1)]).astype(F32)
    all_scales = jnp.concatenate([scales, jnp.where(section == 3, scales2, scales)])
    layer_cost = cost(2 * rows * width * width, 2 * width * width, rows * width)
    out1, cross = pl.pallas_call(
        functools.partial(encoder_kernel, n),
        out_shape=(row_shape, jax.ShapeDtypeStruct((rows, 4 * HEAD), BF16)),
        in_specs=[SMEM] * 3 + [VMEM] + [ANY] * (1 + n),
        out_specs=(VMEM, VMEM),
        scratch_shapes=scratch
        + [
            pltpu.VMEM((3, width, 2 * HEAD), BF16),
            pltpu.SemaphoreType.DMA((3,)),
            pltpu.VMEM((rows, HEAD), BF16),
            pltpu.VMEM((rows, HEAD), BF16),
        ],
        compiler_params=params(),
        cost_estimate=layer_cost,
    )(section, seq_lengths, scales, all_gains, full, *passed)
    cross = hop(cross, [(1, 2)]) + hop(cross, [(1, 3)])

    result = pl.pallas_call(
        functools.partial(decoder_kernel, n),
        out_shape=row_shape,
        in_specs=[SMEM] * 3 + [VMEM, ANY, VMEM, ANY, VMEM] + [ANY] * (2 * n),
        out_specs=VMEM,
        scratch_shapes=scratch + [pltpu.VMEM((rows, width), BF16)],
        compiler_params=params(),
        cost_estimate=layer_cost,
    )(section, seq_lengths, all_scales, wide_gain, full, cross, out1, target2, *made, *passed)
    return result.reshape(1, micro, seqs, length, width), next_part[None]


def solution(mesh):
    in_specs = (
        P("section", "fsdp", None),
        P("section", "fsdp", None),
        P("section", None),
        P("section", None),
        P("section", None, "fsdp"),
        P(None, "fsdp", None, None),
        P(None, "fsdp", None, None),
        P(None, "fsdp"),
    )
    out_specs = (P("section", None, "fsdp", None, None), P("section", None, "fsdp"))
    return jax.shard_map(shards, mesh=mesh, in_specs=in_specs, out_specs=out_specs, check_vma=False)
```

```python
import functools
import math

import jax
import jax.numpy as jnp
from jax import lax
from jax.experimental import pallas as pl
from jax.experimental.pallas import tpu as pltpu
from jax.sharding import PartitionSpec as P

HEAD = 128
EPS = 1e-06
F32 = jnp.float32
BF16 = jnp.bfloat16
VMEM_LIMIT = 48 * 1024 * 1024
BLOCK = 512
PIECES = (512, 1024, 1024, 1024, 512)
SLOTS = 3
LOG2E_SCALED = math.log2(math.e) / math.sqrt(HEAD)
ANY = pl.BlockSpec(memory_space=pl.ANY)
VMEM = pl.BlockSpec(memory_space=pltpu.VMEM)
SMEM = pl.BlockSpec(memory_space=pltpu.SMEM)


def dot(a, b):
    return jnp.dot(a, b, preferred_element_type=F32)


def moves(fn):
    pairs = []
    for index in range(32):
        x, z, core = index // 8, (index // 2) % 4, index % 2
        x2, z2, core2 = fn(x, z, core)
        pairs.append((index, (x2 % 4) * 8 + (z2 % 4) * 2 + core2))
    return pairs


CORE_SWAP = moves(lambda x, z, c: (x, z, 1 - c))
DOUBLING = (
    CORE_SWAP,
    moves(lambda x, z, c: (x, z ^ 1, c)),
    moves(lambda x, z, c: (x ^ 1, z, c)),
    moves(lambda x, z, c: (x, z ^ 2, c)),
    moves(lambda x, z, c: (x ^ 2, z, c)),
)


def send(value, pairs):
    return lax.ppermute(value, "fsdp", pairs)


def total(value):
    for pairs in DOUBLING:
        value = value + send(value, pairs)
    return value


def params():
    return pltpu.CompilerParams(vmem_limit_bytes=VMEM_LIMIT)


def cost(flops, size, exps=0):
    share = 64
    return pl.CostEstimate(flops=int(flops) // share, bytes_accessed=int(size) // share, transcendentals=int(exps) // share)


def half_kernel(core_ref, full_ref, *refs):
    out_ref, sem = refs[-2:]
    rows, width = out_ref.shape
    at = pl.ds(pl.multiple_of(core_ref[0] * rows, rows), rows)
    copy = pltpu.make_async_copy(full_ref.at[at, pl.ds(full_ref.shape[1] - width, width)], out_ref, sem)
    copy.start()
    copy.wait()


def half_rows(full, width, core, *late):
    return pl.pallas_call(
        half_kernel,
        out_shape=jax.ShapeDtypeStruct((full.shape[0] // 2, width), full.dtype),
        in_specs=[SMEM] + [ANY] * (1 + len(late)),
        out_specs=VMEM,
        scratch_shapes=[pltpu.SemaphoreType.DMA],
        compiler_params=params(),
        cost_estimate=cost(0, 0),
    )(core, full, *late)


def copy_kernel(x_ref, *refs):
    refs[-1][...] = x_ref[...]


def copied(x, *late):
    return pl.pallas_call(
        copy_kernel,
        out_shape=jax.ShapeDtypeStruct(x.shape, x.dtype),
        in_specs=[VMEM] + [ANY] * len(late),
        out_specs=VMEM,
        compiler_params=params(),
        cost_estimate=cost(0, 0),
    )(x, *late)


def norm_into(xn_ref, x_ref, gain_ref, row):
    wide = x_ref[...].astype(F32)
    inv = lax.rsqrt(jnp.mean(wide * wide, axis=-1, keepdims=True) + EPS)
    xn_ref[...] = (wide * inv * gain_ref[row : row + 1, :]).astype(BF16)


def attend(q, keys_ref, values_ref, resid, lengths_ref, key_scale, value_scale):
    seqs, heads = q.shape[0] // 128, q.shape[1] // HEAD
    position = lax.broadcasted_iota(jnp.int32, (heads * 128, 128), 1)
    made = []
    for m in range(seqs):
        rows = slice(m * 128, (m + 1) * 128)
        stacked = jnp.concatenate([q[rows, h * HEAD : (h + 1) * HEAD] for h in range(heads)], 0)
        scores = lax.dot_general(
            stacked, keys_ref[rows, :], (((1,), (1,)), ((), ())), preferred_element_type=F32
        )
        expd = jnp.where(position < lengths_ref[m], jnp.exp2(scores * (key_scale * LOG2E_SCALED)), 0.0)
        probs = (expd * (1.0 / jnp.sum(expd, axis=-1, keepdims=True))).astype(BF16)
        context = dot(probs, values_ref[rows, :]) * value_scale
        made.append(jnp.concatenate([context[h * 128 : (h + 1) * 128] for h in range(heads)], 1))
    return (resid.astype(F32) + jnp.concatenate(made, 0)).astype(BF16)


def project_into(keys_ref, values_ref, xn, kv):
    projected = dot(xn, kv).astype(BF16)
    keys_ref[...] = projected[:, :HEAD]
    values_ref[...] = projected[:, HEAD:]


def enter_kernel(section_ref, source_ref, target_ref, gain_ref, x_ref, xn_ref):
    @pl.when(section_ref[0] == 2)
    def _():
        x_ref[...] = target_ref[...]

    @pl.when(section_ref[0] != 2)
    def _():
        x_ref[...] = source_ref[...]

    norm_into(xn_ref, x_ref, gain_ref, 0)


def project_kernel(xn_ref, kv_ref, late_ref, keys_ref, values_ref):
    project_into(keys_ref, values_ref, xn_ref[...], kv_ref[...])


def part_kernel(lengths_ref, section_ref, scale_ref, xn_ref, w_ref, k_ref, v_ref, x_ref, *refs):
    out_ref = refs[-1]
    q = (dot(xn_ref[...], w_ref[...]) * scale_ref[0]).astype(BF16)

    @pl.when(section_ref[0] != 2)
    def _():
        out_ref[...] = attend(q, k_ref, v_ref, x_ref[...], lengths_ref, scale_ref[1], scale_ref[2])

    @pl.when(section_ref[0] == 2)
    def _():
        out_ref[...] = q


def layer_part(xn, full, keys, values, x, at, piece, lengths, section, scales, late):
    rows, width = xn.shape
    first = at // BLOCK
    whole = lambda a: pl.BlockSpec(a.shape, lambda j: (0, 0))
    return pl.pallas_call(
        part_kernel,
        grid=(piece // BLOCK,),
        out_shape=jax.ShapeDtypeStruct((rows, piece), BF16),
        in_specs=[
            SMEM,
            SMEM,
            SMEM,
            whole(xn),
            pl.BlockSpec((width, BLOCK), lambda j: (0, first + j)),
            whole(keys),
            whole(values),
            pl.BlockSpec((rows, BLOCK), lambda j: (0, first + j)),
        ]
        + [ANY] * len(late),
        out_specs=pl.BlockSpec((rows, BLOCK), lambda j: (0, j)),
        compiler_params=params(),
        cost_estimate=cost(2 * rows * width * piece, 2 * width * piece, rows * piece),
    )(lengths, section, scales, xn, full, keys, values, x, *late)


def stream_layer(full, buf, sems, xn_ref, q_ref, k_ref, v_ref, x_ref, lengths_ref, scale_ref, out_ref):
    blocks = x_ref.shape[1] // BLOCK

    def block(b):
        slot = lax.rem(b, SLOTS)
        at = pl.ds(pl.multiple_of(b * BLOCK, BLOCK), BLOCK)
        return pltpu.make_async_copy(full.at[:, at], buf.at[slot], sems.at[slot])

    def start():
        for b in range(SLOTS - 1):
            block(jnp.int32(b)).start()

    def run():
        q_ref[...] = jnp.zeros_like(q_ref)

        def emit(b):
            columns = pl.ds(pl.multiple_of(b * BLOCK, BLOCK), BLOCK)
            out_ref[:, columns] = attend(
                q_ref[...], k_ref, v_ref, x_ref[:, columns], lengths_ref, scale_ref[1], scale_ref[2]
            )

        def step(b, carry):
            slot = lax.rem(b, SLOTS)
            block(b).wait()

            @pl.when(b + SLOTS - 1 < blocks)
            def _():
                block(b + SLOTS - 1).start()

            acc = dot(xn_ref[...], buf[slot])
            emit(jnp.maximum(b - 1, 0))
            q_ref[...] = (acc * scale_ref[0]).astype(BF16)
            return carry

        lax.fori_loop(0, blocks, step, 0)
        emit(jnp.int32(blocks - 1))

    return start, run


def bring(pieces, out_ref, sems):
    at = 0
    copies = []
    for i, piece in enumerate(pieces):
        copies.append(pltpu.make_async_copy(piece, out_ref.at[:, pl.ds(at, piece.shape[1])], sems.at[i]))
        at += piece.shape[1]
    return copies


def encoder_kernel(count, *refs):
    section_ref, core_ref, lengths_ref, scale_ref, gain_ref, full = refs[:6]
    kv_refs, pieces = refs[6:10], refs[10 : 10 + count]
    out_ref, cross_ref = refs[10 + count : 12 + count]
    buf, sems, xn_ref, q_ref, x_ref, x_sems, kv_buf, kv_sems, k_ref, v_ref = refs[12 + count :]
    width = x_ref.shape[1]

    @pl.when(section_ref[0] == 1)
    def _():
        arrive = bring(pieces, x_ref, x_sems)
        for copy in arrive:
            copy.start()
        half = width // 2
        kv_copies = [
            pltpu.make_async_copy(full.at[:, pl.ds(width, 2 * HEAD)], kv_buf.at[0], kv_sems.at[0])
        ]
        for i, ref in enumerate(kv_refs):
            kind = core_ref[0] if i % 2 == 0 else 1 - core_ref[0]
            rows = pl.ds(pl.multiple_of(kind * half, half), half)
            kv_copies.append(
                pltpu.make_async_copy(ref, kv_buf.at[1 + i // 2, rows], kv_sems.at[1 + i])
            )
        for copy in kv_copies[:1]:
            copy.start()
        start, run = stream_layer(
            full, buf, sems, xn_ref, q_ref, k_ref, v_ref, x_ref, lengths_ref, scale_ref, out_ref
        )
        start()
        for copy in kv_copies[1:]:
            copy.start()
        for copy in arrive:
            copy.wait()
        norm_into(xn_ref, x_ref, gain_ref, 0)
        for copy in kv_copies[:1]:
            copy.wait()
        project_into(k_ref, v_ref, xn_ref[...], kv_buf[0])
        run()
        for copy in kv_copies[1:]:
            copy.wait()
        for i in (1, 2):
            norm_into(xn_ref, out_ref, gain_ref, i)
            at = (i - 1) * 2 * HEAD
            project_into(
                cross_ref.at[:, pl.ds(at, HEAD)],
                cross_ref.at[:, pl.ds(at + HEAD, HEAD)],
                xn_ref[...],
                kv_buf[i],
            )


def decoder_kernel(count, *refs):
    section_ref, lengths_ref, scale_ref, gain_ref, full, cross_ref, first_out, target = refs[:8]
    made, passed = refs[8 : 8 + count], refs[8 + count : 8 + 2 * count]
    out_ref = refs[8 + 2 * count]
    buf, sems, xn_ref, q_ref, x_ref, x_sems, mid_ref = refs[9 + 2 * count :]
    section = section_ref[0]
    blocks = x_ref.shape[1] // BLOCK
    cols = lambda i: cross_ref.at[:, pl.ds(i * HEAD, HEAD)]

    def fetch(pieces, into):
        copies = bring(pieces, into, x_sems)
        for copy in copies:
            copy.start()
        for copy in copies:
            copy.wait()

    def attend_all(resid_ref, into):
        def step(b, carry):
            columns = pl.ds(pl.multiple_of(b * BLOCK, BLOCK), BLOCK)
            into[:, columns] = attend(
                x_ref[:, columns], cols(0), cols(1), resid_ref[:, columns], lengths_ref, scale_ref[4], scale_ref[5]
            )
            return carry

        lax.fori_loop(0, blocks, step, 0)

    @pl.when(section == 0)
    def _():
        fetch(made, out_ref)

    @pl.when(section == 1)
    def _():
        fetch([first_out], out_ref)

    @pl.when(section == 2)
    def _():
        fetch(made, x_ref)
        attend_all(target, out_ref)

    @pl.when(section == 3)
    def _():
        start, run = stream_layer(
            full, buf, sems, xn_ref, q_ref, cols(2), cols(3), mid_ref, lengths_ref, scale_ref, out_ref
        )
        copies = bring(passed, x_ref, x_sems)
        for copy in copies:
            copy.start()
        start()
        for copy in copies:
            copy.wait()
        attend_all(target, mid_ref)
        norm_into(xn_ref, mid_ref, gain_ref, 0)
        run()


def unit_direction(along):
    return (along * lax.rsqrt(jnp.sum(along * along) + EPS)).astype(BF16)


def spectral_along(weight, kv_part, start_rows):
    of_kv = dot(start_rows, kv_part)
    parts = jnp.concatenate([dot(start_rows[0:1], weight)[0], of_kv[1, :HEAD], of_kv[2, HEAD:]])
    return total(parts.reshape(-1, 128))


def spectral_images(weight, kv_part, along):
    width = weight.shape[1]
    return jnp.stack(
        [
            dot(weight, unit_direction(along[:width])),
            dot(kv_part[:, :HEAD], unit_direction(along[width : width + HEAD])),
            dot(kv_part[:, HEAD:], unit_direction(along[width + HEAD :])),
        ]
    )


def shards(weights, kv_weights, gammas, gains, starts, source, target, lengths):
    weight, kv_part, gamma, gain, start_rows = weights[0], kv_weights[0], gammas[0], gains[0], starts[0]
    width = weight.shape[1]
    section = lax.axis_index("section").astype(jnp.int32).reshape(1)
    micro, seqs, length, _ = source.shape
    rows = micro * seqs * length
    seq_lengths = lengths.reshape(-1)
    source2 = source.reshape(rows, width)
    target2 = target.reshape(rows, width)
    wide_gain = gain.astype(F32).reshape(1, width)
    row_shape = jax.ShapeDtypeStruct((rows, width), BF16)
    head_shape = jax.ShapeDtypeStruct((rows, HEAD), BF16)

    hop = lambda value, pairs: lax.ppermute(value, "section", pairs)

    full = lax.all_gather(jnp.concatenate([weight, kv_part], 1), "fsdp", axis=0, tiled=True)

    gain_rows = gain.reshape(-1, 128)
    gain2 = hop(gain_rows, [(2, 1)])
    gain3 = hop(gain_rows, [(3, 1)])
    along = spectral_along(weight, kv_part, start_rows).reshape(-1)
    images = spectral_images(weight, kv_part, along)
    squares = jnp.broadcast_to(jnp.sum(images * images, axis=1)[:, None], (3, 128))
    sigmas = jnp.sqrt(total(squares)[:, 0] + EPS)
    scales, next_part = gamma / sigmas, images / sigmas[:, None]
    scales2 = hop(jnp.broadcast_to(scales[:, None], (3, 128)), [(2, 3)])[:, 0]

    x0, xn0 = pl.pallas_call(
        enter_kernel,
        out_shape=(row_shape, row_shape),
        in_specs=[SMEM, VMEM, VMEM, VMEM],
        out_specs=(VMEM, VMEM),
        compiler_params=params(),
        cost_estimate=cost(8 * rows * width, 8 * rows * width),
    )(section, source2, target2, wide_gain)

    core = lax.rem(lax.axis_index("fsdp"), 2).astype(jnp.int32).reshape(1)
    kv_half = half_rows(full, 2 * HEAD, core, scales, scales2, gain2, gain3, xn0)
    kv2 = hop(kv_half, [(3, 2), (2, 1)])

    kv_block = pl.BlockSpec((width, 2 * HEAD), lambda j: (0, width // (2 * HEAD)))
    whole = lambda shape: pl.BlockSpec(shape, lambda j: (0, 0))
    keys, values = pl.pallas_call(
        project_kernel,
        grid=(1,),
        out_shape=(head_shape, head_shape),
        in_specs=[whole((rows, width)), kv_block, ANY],
        out_specs=(whole((rows, HEAD)), whole((rows, HEAD))),
        compiler_params=params(),
        cost_estimate=cost(4 * rows * width * HEAD, 4 * width * HEAD),
    )(xn0, full, kv_half)

    made, passed = [], []
    at = 0
    for i, piece in enumerate(PIECES):
        late = made[-1:] + (passed[i - 2 : i - 1] if i >= 2 else [])
        made.append(layer_part(xn0, full, keys, values, x0, at, piece, seq_lengths, section, scales, late))
        passed.append(hop(made[-1], [(0, 1), (2, 3)]))
        at += piece
        if i == 2:
            kv2 = copied(kv2, made[-1], passed[1])
            kv3 = hop(kv2, [(2, 1)])
    kv3 = copied(kv3, made[-1], passed[3])
    kv_halves = [kv2, send(kv2, CORE_SWAP), kv3, send(kv3, CORE_SWAP)]

    scratch = [
        pltpu.VMEM((SLOTS, width, BLOCK), BF16),
        pltpu.SemaphoreType.DMA((SLOTS,)),
        pltpu.VMEM((rows, width), BF16),
        pltpu.VMEM((rows, BLOCK), BF16),
        pltpu.VMEM((rows, width), BF16),
        pltpu.SemaphoreType.DMA((len(made),)),
    ]
    n = len(made)
    all_gains = jnp.concatenate([gain[None], gain2.reshape(1, width), gain3.reshape(1, width)], 0).astype(F32)
    all_scales = jnp.concatenate([scales, jnp.where(section == 3, scales2, scales)])
    layer_cost = cost(2 * rows * width * width, 2 * width * width, rows * width)
    out1, cross = pl.pallas_call(
        functools.partial(encoder_kernel, n),
        out_shape=(row_shape, jax.ShapeDtypeStruct((rows, 4 * HEAD), BF16)),
        in_specs=[SMEM] * 4 + [VMEM] + [ANY] * (5 + n),
        out_specs=(VMEM, VMEM),
        scratch_shapes=scratch
        + [
            pltpu.VMEM((3, width, 2 * HEAD), BF16),
            pltpu.SemaphoreType.DMA((5,)),
            pltpu.VMEM((rows, HEAD), BF16),
            pltpu.VMEM((rows, HEAD), BF16),
        ],
        compiler_params=params(),
        cost_estimate=layer_cost,
    )(section, core, seq_lengths, scales, all_gains, full, *kv_halves, *passed)
    cross = hop(cross, [(1, 2)]) + hop(cross, [(1, 3)])

    result = pl.pallas_call(
        functools.partial(decoder_kernel, n),
        out_shape=row_shape,
        in_specs=[SMEM] * 3 + [VMEM, ANY, VMEM, ANY, VMEM] + [ANY] * (2 * n),
        out_specs=VMEM,
        scratch_shapes=scratch + [pltpu.VMEM((rows, width), BF16)],
        compiler_params=params(),
        cost_estimate=layer_cost,
    )(section, seq_lengths, all_scales, wide_gain, full, cross, out1, target2, *made, *passed)
    return result.reshape(1, micro, seqs, length, width), next_part[None]


def solution(mesh):
    in_specs = (
        P("section", "fsdp", None),
        P("section", "fsdp", None),
        P("section", None),
        P("section", None),
        P("section", None, "fsdp"),
        P(None, "fsdp", None, None),
        P(None, "fsdp", None, None),
        P(None, "fsdp"),
    )
    out_specs = (P("section", None, "fsdp", None, None), P("section", None, "fsdp"))
    return jax.shard_map(shards, mesh=mesh, in_specs=in_specs, out_specs=out_specs, check_vma=False)
```

```python
import functools
import math

import jax
import jax.numpy as jnp
from jax import lax
from jax.experimental import pallas as pl
from jax.experimental.pallas import tpu as pltpu
from jax.sharding import PartitionSpec as P

HEAD = 128
EPS = 1e-06
F32 = jnp.float32
BF16 = jnp.bfloat16
VMEM_LIMIT = 48 * 1024 * 1024
BLOCK = 512
PIECE = 1024
SLOTS = 3
LOG2E_SCALED = math.log2(math.e) / math.sqrt(HEAD)
ANY = pl.BlockSpec(memory_space=pl.ANY)
VMEM = pl.BlockSpec(memory_space=pltpu.VMEM)
SMEM = pl.BlockSpec(memory_space=pltpu.SMEM)


def dot(a, b):
    return jnp.dot(a, b, preferred_element_type=F32)


def moves(fn):
    pairs = []
    for index in range(32):
        x, z, core = index // 8, (index // 2) % 4, index % 2
        x2, z2, core2 = fn(x, z, core)
        pairs.append((index, (x2 % 4) * 8 + (z2 % 4) * 2 + core2))
    return pairs


ROUTE = (0, -1, 1, 2)
CORE_SWAP = moves(lambda x, z, c: (x, z, 1 - c))
DOUBLING = (
    CORE_SWAP,
    moves(lambda x, z, c: (x, z ^ 1, c)),
    moves(lambda x, z, c: (x ^ 1, z, c)),
    moves(lambda x, z, c: (x, z ^ 2, c)),
    moves(lambda x, z, c: (x ^ 2, z, c)),
)


def send(value, pairs):
    return lax.ppermute(value, "fsdp", pairs)


def along_first(step):
    return moves(lambda x, z, c: (x, z + step, c) if c == 0 else (x + step, z, c))


def along_second(step):
    return moves(lambda x, z, c: (x + step, z, c) if c == 0 else (x, z + step, c))


def send_one(value, pairs):
    return lax.ppermute(value, ("section", "fsdp"), [(32 + a, 32 + b) for a, b in pairs])


def ring(block, move):
    before, after = send_one(block, move(1)), send_one(block, move(-1))
    return [block, before, after, send_one(before, move(1))]


def row_order():
    index = lax.axis_index("fsdp")
    x, z, core = index // 8, (index // 2) % 4, index % 2
    first = jnp.array(ROUTE, jnp.int32)
    line, plane = jnp.tile(first, 4), jnp.repeat(first, 4)

    def order(kind):
        zs = z + jnp.where(kind == 0, line, plane)
        xs = x + jnp.where(kind == 0, plane, line)
        return ((xs + 8) % 4) * 8 + ((zs + 8) % 4) * 2 + kind

    return jnp.concatenate([order(core), order(1 - core)]).astype(jnp.int32)


def total(value):
    for pairs in DOUBLING:
        value = value + send(value, pairs)
    return value


def params():
    return pltpu.CompilerParams(vmem_limit_bytes=VMEM_LIMIT)


def cost(flops, size, exps=0):
    share = 64
    return pl.CostEstimate(flops=int(flops) // share, bytes_accessed=int(size) // share, transcendentals=int(exps) // share)


def stack_kernel(count, *refs):
    sources, out, held, sems = refs[:count], refs[count], refs[count + 1], refs[count + 2]
    rows = sources[0].shape[0]
    reads = [pltpu.make_async_copy(source, held.at[i], sems.at[0, i]) for i, source in enumerate(sources)]
    writes = [
        pltpu.make_async_copy(held.at[i], out.at[pl.ds(i * rows, rows)], sems.at[1, i]) for i in range(count)
    ]
    for read in reads:
        read.start()
    for read, write in zip(reads, writes):
        read.wait()
        write.start()
    for write in writes:
        write.wait()


def stack(blocks):
    count = len(blocks)
    rows, width = blocks[0].shape
    return pl.pallas_call(
        functools.partial(stack_kernel, count),
        out_shape=jax.ShapeDtypeStruct((count * rows, width), blocks[0].dtype),
        in_specs=[ANY] * count,
        out_specs=ANY,
        scratch_shapes=[pltpu.VMEM((count, rows, width), blocks[0].dtype), pltpu.SemaphoreType.DMA((2, count))],
        compiler_params=pltpu.CompilerParams(vmem_limit_bytes=12 * 1024 * 1024),
        cost_estimate=cost(0, 4 * count * rows * width),
    )(*blocks)


def norm_into(xn_ref, x_ref, gain_ref, row):
    wide = x_ref[...].astype(F32)
    inv = lax.rsqrt(jnp.mean(wide * wide, axis=-1, keepdims=True) + EPS)
    xn_ref[...] = (wide * inv * gain_ref[row : row + 1, :]).astype(BF16)


def attend(q, keys_ref, values_ref, resid, lengths_ref, key_scale, value_scale):
    seqs, heads = q.shape[0] // 128, q.shape[1] // HEAD
    position = lax.broadcasted_iota(jnp.int32, (heads * 128, 128), 1)
    made = []
    for m in range(seqs):
        rows = slice(m * 128, (m + 1) * 128)
        stacked = jnp.concatenate([q[rows, h * HEAD : (h + 1) * HEAD] for h in range(heads)], 0)
        scores = lax.dot_general(
            stacked, keys_ref[rows, :], (((1,), (1,)), ((), ())), preferred_element_type=F32
        )
        expd = jnp.where(position < lengths_ref[m], jnp.exp2(scores * (key_scale * LOG2E_SCALED)), 0.0)
        probs = (expd * (1.0 / jnp.sum(expd, axis=-1, keepdims=True))).astype(BF16)
        context = dot(probs, values_ref[rows, :]) * value_scale
        made.append(jnp.concatenate([context[h * 128 : (h + 1) * 128] for h in range(heads)], 1))
    return (resid.astype(F32) + jnp.concatenate(made, 0)).astype(BF16)


def project_into(keys_ref, values_ref, xn, kv):
    projected = dot(xn, kv).astype(BF16)
    keys_ref[...] = projected[:, :HEAD]
    values_ref[...] = projected[:, HEAD:]


def enter_kernel(section_ref, source_ref, target_ref, gain_ref, x_ref, xn_ref):
    @pl.when(section_ref[0] == 2)
    def _():
        x_ref[...] = target_ref[...]

    @pl.when(section_ref[0] != 2)
    def _():
        x_ref[...] = source_ref[...]

    norm_into(xn_ref, x_ref, gain_ref, 0)


def project_kernel(xn_ref, kv_ref, *refs):
    keys_ref, values_ref = refs[-2:]
    project_into(keys_ref, values_ref, xn_ref[...], kv_ref[...])


def part_kernel(lengths_ref, section_ref, scale_ref, xn_ref, w_ref, k_ref, v_ref, x_ref, out_ref):
    query = lambda: (dot(xn_ref[...], w_ref[...]) * scale_ref[0]).astype(BF16)

    @pl.when(section_ref[0] == 0)
    def _():
        out_ref[...] = attend(query(), k_ref, v_ref, x_ref[...], lengths_ref, scale_ref[1], scale_ref[2])

    @pl.when(section_ref[0] == 2)
    def _():
        out_ref[...] = query()

    @pl.when(lax.rem(section_ref[0], 2) == 1)
    def _():
        out_ref[...] = jnp.zeros_like(out_ref)


def layer_part(xn, full, keys, values, x, at, lengths, section, scales):
    rows, width = xn.shape
    first = at // BLOCK
    whole = lambda a: pl.BlockSpec(a.shape, lambda j: (0, 0))
    return pl.pallas_call(
        part_kernel,
        grid=(PIECE // BLOCK,),
        out_shape=jax.ShapeDtypeStruct((rows, PIECE), BF16),
        in_specs=[
            SMEM,
            SMEM,
            SMEM,
            whole(xn),
            pl.BlockSpec((width, BLOCK), lambda j: (0, first + j)),
            whole(keys),
            whole(values),
            pl.BlockSpec((rows, BLOCK), lambda j: (0, first + j)),
        ],
        out_specs=pl.BlockSpec((rows, BLOCK), lambda j: (0, j)),
        compiler_params=params(),
        cost_estimate=cost(2 * rows * width * PIECE, 2 * width * PIECE, rows * PIECE),
    )(lengths, section, scales, xn, full, keys, values, x)


def stream_layer(full, buf, sems, xn_ref, q_ref, k_ref, v_ref, x_ref, lengths_ref, scale_ref, out_ref):
    blocks = x_ref.shape[1] // BLOCK

    def block(b):
        slot = lax.rem(b, SLOTS)
        at = pl.ds(pl.multiple_of(b * BLOCK, BLOCK), BLOCK)
        return pltpu.make_async_copy(full.at[:, at], buf.at[slot], sems.at[slot])

    def start():
        for b in range(SLOTS - 1):
            block(jnp.int32(b)).start()

    def run():
        q_ref[...] = jnp.zeros_like(q_ref)

        def emit(b):
            columns = pl.ds(pl.multiple_of(b * BLOCK, BLOCK), BLOCK)
            out_ref[:, columns] = attend(
                q_ref[...], k_ref, v_ref, x_ref[:, columns], lengths_ref, scale_ref[1], scale_ref[2]
            )

        def step(b, carry):
            slot = lax.rem(b, SLOTS)
            block(b).wait()

            @pl.when(b + SLOTS - 1 < blocks)
            def _():
                block(b + SLOTS - 1).start()

            acc = dot(xn_ref[...], buf[slot])
            emit(jnp.maximum(b - 1, 0))
            q_ref[...] = (acc * scale_ref[0]).astype(BF16)
            return carry

        lax.fori_loop(0, blocks, step, 0)
        emit(jnp.int32(blocks - 1))

    return start, run


def bring(pieces, out_ref, sems):
    at = 0
    copies = []
    for i, piece in enumerate(pieces):
        copies.append(pltpu.make_async_copy(piece, out_ref.at[:, pl.ds(at, piece.shape[1])], sems.at[i]))
        at += piece.shape[1]
    return copies


def encoder_kernel(count, *refs):
    section_ref, order_ref, lengths_ref, scale_ref, gain_ref, full = refs[:6]
    kv_refs, pieces = refs[6:8], refs[8 : 8 + count]
    out_ref, cross_ref = refs[8 + count : 10 + count]
    buf, sems, xn_ref, q_ref, x_ref, x_sems, kv_buf, kv_sems, k_ref, v_ref = refs[10 + count :]
    width = x_ref.shape[1]

    @pl.when(section_ref[0] == 1)
    def _():
        arrive = bring(pieces, x_ref, x_sems)
        for copy in arrive:
            copy.start()
        of_layer = lambda i: pltpu.make_async_copy(
            full.at[:, pl.ds(width, 2 * HEAD)], kv_buf.at[i], kv_sems.at[i]
        )

        def begin_later():
            for k in range(32):
                ref, row = kv_refs[k // 16], k % 16 * 128
                rows = pl.ds(pl.multiple_of(order_ref[k] * 128, 128), 128)
                for i in (1, 2):
                    block = ref.at[pl.ds(row, 128), pl.ds((i - 1) * 2 * HEAD, 2 * HEAD)]
                    pltpu.make_async_copy(block, kv_buf.at[i, rows], kv_sems.at[i]).start()

        of_layer(0).start()
        start, run = stream_layer(
            full, buf, sems, xn_ref, q_ref, k_ref, v_ref, x_ref, lengths_ref, scale_ref, out_ref
        )
        start()
        begin_later()
        for copy in arrive:
            copy.wait()
        norm_into(xn_ref, x_ref, gain_ref, 0)
        of_layer(0).wait()
        project_into(k_ref, v_ref, xn_ref[...], kv_buf[0])
        run()
        for i in (1, 2):
            of_layer(i).wait()
        for i in (1, 2):
            norm_into(xn_ref, out_ref, gain_ref, i)
            at = (i - 1) * 2 * HEAD
            project_into(
                cross_ref.at[:, pl.ds(at, HEAD)],
                cross_ref.at[:, pl.ds(at + HEAD, HEAD)],
                xn_ref[...],
                kv_buf[i],
            )


def decoder_kernel(count, *refs):
    section_ref, lengths_ref, scale_ref, gain_ref, full, cross_ref, first_out, target = refs[:8]
    made, passed = refs[8 : 8 + count], refs[8 + count : 8 + 2 * count]
    out_ref = refs[8 + 2 * count]
    buf, sems, xn_ref, q_ref, x_ref, x_sems, mid_ref = refs[9 + 2 * count :]
    section = section_ref[0]
    blocks = x_ref.shape[1] // BLOCK
    cols = lambda i: cross_ref.at[:, pl.ds(i * HEAD, HEAD)]

    def fetch(pieces, into):
        copies = bring(pieces, into, x_sems)
        for copy in copies:
            copy.start()
        for copy in copies:
            copy.wait()

    def attend_all(resid_ref, into):
        def step(b, carry):
            columns = pl.ds(pl.multiple_of(b * BLOCK, BLOCK), BLOCK)
            into[:, columns] = attend(
                x_ref[:, columns], cols(0), cols(1), resid_ref[:, columns], lengths_ref, scale_ref[4], scale_ref[5]
            )
            return carry

        lax.fori_loop(0, blocks, step, 0)

    @pl.when(section == 0)
    def _():
        fetch(made, out_ref)

    @pl.when(section == 1)
    def _():
        fetch([first_out], out_ref)

    @pl.when(section == 2)
    def _():
        fetch(made, x_ref)
        attend_all(target, out_ref)

    @pl.when(section == 3)
    def _():
        start, run = stream_layer(
            full, buf, sems, xn_ref, q_ref, cols(2), cols(3), mid_ref, lengths_ref, scale_ref, out_ref
        )
        copies = bring(passed, x_ref, x_sems)
        for copy in copies:
            copy.start()
        start()
        for copy in copies:
            copy.wait()
        attend_all(target, mid_ref)
        norm_into(xn_ref, mid_ref, gain_ref, 0)
        run()


def unit_direction(along):
    return (along * lax.rsqrt(jnp.sum(along * along) + EPS)).astype(BF16)


def spectral_along(weight, kv_part, start_rows):
    of_kv = dot(start_rows, kv_part)
    parts = jnp.concatenate([dot(start_rows[0:1], weight)[0], of_kv[1, :HEAD], of_kv[2, HEAD:]])
    return total(parts.reshape(-1, 128))


def spectral_images(weight, kv_part, along):
    width = weight.shape[1]
    return jnp.stack(
        [
            dot(weight, unit_direction(along[:width])),
            dot(kv_part[:, :HEAD], unit_direction(along[width : width + HEAD])),
            dot(kv_part[:, HEAD:], unit_direction(along[width + HEAD :])),
        ]
    )


def shards(weights, kv_weights, gammas, gains, starts, source, target, lengths):
    weight, kv_part, gamma, gain, start_rows = weights[0], kv_weights[0], gammas[0], gains[0], starts[0]
    width = weight.shape[1]
    section = lax.axis_index("section").astype(jnp.int32).reshape(1)
    micro, seqs, length, _ = source.shape
    rows = micro * seqs * length
    seq_lengths = lengths.reshape(-1)
    source2 = source.reshape(rows, width)
    target2 = target.reshape(rows, width)
    wide_gain = gain.astype(F32).reshape(1, width)
    row_shape = jax.ShapeDtypeStruct((rows, width), BF16)
    head_shape = jax.ShapeDtypeStruct((rows, HEAD), BF16)

    hop = lambda value, pairs: lax.ppermute(value, "section", pairs)

    extra = jnp.concatenate([kv_part, gain.reshape(-1, 2 * HEAD)], 0)
    extra2 = hop(extra, [(2, 1)])
    extra3 = hop(extra, [(3, 1)])
    local = kv_part.shape[0]

    line = stack(ring(jnp.concatenate([extra2[:local], extra3[:local]], 1), along_first))
    kv_own = stack(ring(line, along_second))
    kv_other = send_one(kv_own, CORE_SWAP)
    full = lax.all_gather(jnp.concatenate([weight, kv_part], 1), "fsdp", axis=0, tiled=True)

    along = spectral_along(weight, kv_part, start_rows).reshape(-1)
    images = spectral_images(weight, kv_part, along)
    squares = jnp.broadcast_to(jnp.sum(images * images, axis=1)[:, None], (3, 128))
    sigmas = jnp.sqrt(total(squares)[:, 0] + EPS)
    scales, next_part = gamma / sigmas, images / sigmas[:, None]
    scales2 = hop(jnp.broadcast_to(scales[:, None], (3, 128)), [(2, 3)])[:, 0]

    x0, xn0 = pl.pallas_call(
        enter_kernel,
        out_shape=(row_shape, row_shape),
        in_specs=[SMEM, VMEM, VMEM, VMEM],
        out_specs=(VMEM, VMEM),
        compiler_params=params(),
        cost_estimate=cost(8 * rows * width, 8 * rows * width),
    )(section, source2, target2, wide_gain)

    kv_block = pl.BlockSpec((width, 2 * HEAD), lambda j: (0, width // (2 * HEAD)))
    whole = lambda shape: pl.BlockSpec(shape, lambda j: (0, 0))
    keys, values = pl.pallas_call(
        project_kernel,
        grid=(1,),
        out_shape=(head_shape, head_shape),
        in_specs=[whole((rows, width)), kv_block, ANY, ANY],
        out_specs=(whole((rows, HEAD)), whole((rows, HEAD))),
        compiler_params=params(),
        cost_estimate=cost(4 * rows * width * HEAD, 4 * width * HEAD),
    )(xn0, full, kv_own, kv_other)

    made, passed = [], []
    for at in range(0, width, PIECE):
        made.append(layer_part(xn0, full, keys, values, x0, at, seq_lengths, section, scales))
        passed.append(hop(made[-1], [(0, 1), (2, 3)]))

    scratch = [
        pltpu.VMEM((SLOTS, width, BLOCK), BF16),
        pltpu.SemaphoreType.DMA((SLOTS,)),
        pltpu.VMEM((rows, width), BF16),
        pltpu.VMEM((rows, BLOCK), BF16),
        pltpu.VMEM((rows, width), BF16),
        pltpu.SemaphoreType.DMA((len(made),)),
    ]
    n = len(made)
    all_gains = jnp.stack([gain, extra2[local:].reshape(-1), extra3[local:].reshape(-1)]).astype(F32)
    all_scales = jnp.concatenate([scales, jnp.where(section == 3, scales2, scales)])
    layer_cost = cost(2 * rows * width * width, 2 * width * width, rows * width)
    out1, cross = pl.pallas_call(
        functools.partial(encoder_kernel, n),
        out_shape=(row_shape, jax.ShapeDtypeStruct((rows, 4 * HEAD), BF16)),
        in_specs=[SMEM] * 4 + [VMEM] + [ANY] * (3 + n),
        out_specs=(VMEM, VMEM),
        scratch_shapes=scratch
        + [
            pltpu.VMEM((3, width, 2 * HEAD), BF16),
            pltpu.SemaphoreType.DMA((3,)),
            pltpu.VMEM((rows, HEAD), BF16),
            pltpu.VMEM((rows, HEAD), BF16),
        ],
        compiler_params=params(),
        cost_estimate=layer_cost,
    )(section, row_order(), seq_lengths, scales, all_gains, full, kv_own, kv_other, *passed)
    cross = hop(cross, [(1, 2)]) + hop(cross, [(1, 3)])

    result = pl.pallas_call(
        functools.partial(decoder_kernel, n),
        out_shape=row_shape,
        in_specs=[SMEM] * 3 + [VMEM, ANY, VMEM, ANY, VMEM] + [ANY] * (2 * n),
        out_specs=VMEM,
        scratch_shapes=scratch + [pltpu.VMEM((rows, width), BF16)],
        compiler_params=params(),
        cost_estimate=layer_cost,
    )(section, seq_lengths, all_scales, wide_gain, full, cross, out1, target2, *made, *passed)
    return result.reshape(1, micro, seqs, length, width), next_part[None]


def solution(mesh):
    in_specs = (
        P("section", "fsdp", None),
        P("section", "fsdp", None),
        P("section", None),
        P("section", None),
        P("section", None, "fsdp"),
        P(None, "fsdp", None, None),
        P(None, "fsdp", None, None),
        P(None, "fsdp"),
    )
    out_specs = (P("section", None, "fsdp", None, None), P("section", None, "fsdp"))
    return jax.shard_map(shards, mesh=mesh, in_specs=in_specs, out_specs=out_specs, check_vma=False)
```

```python
import functools
import math

import jax
import jax.numpy as jnp
from jax import lax
from jax.experimental import pallas as pl
from jax.experimental.pallas import tpu as pltpu
from jax.sharding import PartitionSpec as P

HEAD = 128
EPS = 1e-06
F32 = jnp.float32
BF16 = jnp.bfloat16
VMEM_LIMIT = 48 * 1024 * 1024
BLOCK = 512
PIECE = 1024
SLOTS = 3
LOG2E_SCALED = math.log2(math.e) / math.sqrt(HEAD)
ANY = pl.BlockSpec(memory_space=pl.ANY)
VMEM = pl.BlockSpec(memory_space=pltpu.VMEM)
SMEM = pl.BlockSpec(memory_space=pltpu.SMEM)


def dot(a, b):
    return jnp.dot(a, b, preferred_element_type=F32)


def moves(fn):
    pairs = []
    for index in range(32):
        x, z, core = index // 8, (index // 2) % 4, index % 2
        x2, z2, core2 = fn(x, z, core)
        pairs.append((index, (x2 % 4) * 8 + (z2 % 4) * 2 + core2))
    return pairs


ROUTE = (0, -1, 1, 2)
CORE_SWAP = moves(lambda x, z, c: (x, z, 1 - c))
DOUBLING = (
    CORE_SWAP,
    moves(lambda x, z, c: (x, z ^ 1, c)),
    moves(lambda x, z, c: (x ^ 1, z, c)),
    moves(lambda x, z, c: (x, z ^ 2, c)),
    moves(lambda x, z, c: (x ^ 2, z, c)),
)


def send(value, pairs):
    return lax.ppermute(value, "fsdp", pairs)


def along_first(step):
    return moves(lambda x, z, c: (x, z + step, c) if c == 0 else (x + step, z, c))


def along_second(step):
    return moves(lambda x, z, c: (x + step, z, c) if c == 0 else (x, z + step, c))


def send_one(value, pairs):
    return lax.ppermute(value, ("section", "fsdp"), [(32 + a, 32 + b) for a, b in pairs])


def ring(block, move):
    before, after = send_one(block, move(1)), send_one(block, move(-1))
    return [block, before, after, send_one(before, move(1))]


def row_order():
    index = lax.axis_index("fsdp")
    x, z, core = index // 8, (index // 2) % 4, index % 2
    first = jnp.array(ROUTE, jnp.int32)
    line, plane = jnp.tile(first, 4), jnp.repeat(first, 4)

    def order(kind):
        zs = z + jnp.where(kind == 0, line, plane)
        xs = x + jnp.where(kind == 0, plane, line)
        return ((xs + 8) % 4) * 8 + ((zs + 8) % 4) * 2 + kind

    return jnp.concatenate([order(core), order(1 - core)]).astype(jnp.int32)


def total(value):
    for pairs in DOUBLING:
        value = value + send(value, pairs)
    return value


def params():
    return pltpu.CompilerParams(vmem_limit_bytes=VMEM_LIMIT)


def cost(flops, size, exps=0):
    share = 64
    return pl.CostEstimate(flops=int(flops) // share, bytes_accessed=int(size) // share, transcendentals=int(exps) // share)


def stack_kernel(count, *refs):
    sources, out, held, sems = refs[:count], refs[count], refs[count + 1], refs[count + 2]
    rows = sources[0].shape[0]
    reads = [pltpu.make_async_copy(source, held.at[i], sems.at[0, i]) for i, source in enumerate(sources)]
    writes = [
        pltpu.make_async_copy(held.at[i], out.at[pl.ds(i * rows, rows)], sems.at[1, i]) for i in range(count)
    ]
    for read in reads:
        read.start()
    for read, write in zip(reads, writes):
        read.wait()
        write.start()
    for write in writes:
        write.wait()


def stack(blocks):
    count = len(blocks)
    rows, width = blocks[0].shape
    return pl.pallas_call(
        functools.partial(stack_kernel, count),
        out_shape=jax.ShapeDtypeStruct((count * rows, width), blocks[0].dtype),
        in_specs=[ANY] * count,
        out_specs=ANY,
        scratch_shapes=[pltpu.VMEM((count, rows, width), blocks[0].dtype), pltpu.SemaphoreType.DMA((2, count))],
        compiler_params=pltpu.CompilerParams(vmem_limit_bytes=12 * 1024 * 1024),
        cost_estimate=cost(0, 4 * count * rows * width),
    )(*blocks)


def inverse_norm(wide):
    return lax.rsqrt(jnp.mean(wide * wide, axis=-1, keepdims=True) + EPS)


def norm_into(xn_ref, x_ref, gain_ref, row):
    wide = x_ref[...].astype(F32)
    xn_ref[...] = (wide * inverse_norm(wide) * gain_ref[row : row + 1, :]).astype(BF16)


def attend(q, keys_ref, values_ref, resid, lengths_ref, key_scale, value_scale):
    seqs, heads = q.shape[0] // 128, q.shape[1] // HEAD
    position = lax.broadcasted_iota(jnp.int32, (heads * 128, 128), 1)
    made = []
    for m in range(seqs):
        rows = slice(m * 128, (m + 1) * 128)
        stacked = jnp.concatenate([q[rows, h * HEAD : (h + 1) * HEAD] for h in range(heads)], 0)
        scores = lax.dot_general(
            stacked, keys_ref[rows, :], (((1,), (1,)), ((), ())), preferred_element_type=F32
        )
        expd = jnp.where(position < lengths_ref[m], jnp.exp2(scores * (key_scale * LOG2E_SCALED)), 0.0)
        probs = (expd * (1.0 / jnp.sum(expd, axis=-1, keepdims=True))).astype(BF16)
        context = dot(probs, values_ref[rows, :]) * value_scale
        made.append(jnp.concatenate([context[h * 128 : (h + 1) * 128] for h in range(heads)], 1))
    return (resid.astype(F32) + jnp.concatenate(made, 0)).astype(BF16)


def project_into(keys_ref, values_ref, xn, kv):
    projected = dot(xn, kv).astype(BF16)
    keys_ref[...] = projected[:, :HEAD]
    values_ref[...] = projected[:, HEAD:]


def enter_kernel(section_ref, source_ref, target_ref, gain_ref, x_ref, xn_ref):
    @pl.when(section_ref[0] == 2)
    def _():
        x_ref[...] = target_ref[...]

    @pl.when(section_ref[0] != 2)
    def _():
        x_ref[...] = source_ref[...]

    norm_into(xn_ref, x_ref, gain_ref, 0)


def project_kernel(xn_ref, kv_ref, *refs):
    keys_ref, values_ref = refs[-2:]
    project_into(keys_ref, values_ref, xn_ref[...], kv_ref[...])


def part_kernel(lengths_ref, section_ref, scale_ref, xn_ref, w_ref, k_ref, v_ref, x_ref, out_ref):
    query = lambda: (dot(xn_ref[...], w_ref[...]) * scale_ref[0]).astype(BF16)

    @pl.when(section_ref[0] == 0)
    def _():
        out_ref[...] = attend(query(), k_ref, v_ref, x_ref[...], lengths_ref, scale_ref[1], scale_ref[2])

    @pl.when(section_ref[0] == 2)
    def _():
        out_ref[...] = query()

    @pl.when(lax.rem(section_ref[0], 2) == 1)
    def _():
        out_ref[...] = jnp.zeros_like(out_ref)


def layer_part(xn, full, keys, values, x, at, lengths, section, scales):
    rows, width = xn.shape
    first = at // BLOCK
    whole = lambda a: pl.BlockSpec(a.shape, lambda j: (0, 0))
    return pl.pallas_call(
        part_kernel,
        grid=(PIECE // BLOCK,),
        out_shape=jax.ShapeDtypeStruct((rows, PIECE), BF16),
        in_specs=[
            SMEM,
            SMEM,
            SMEM,
            whole(xn),
            pl.BlockSpec((width, BLOCK), lambda j: (0, first + j)),
            whole(keys),
            whole(values),
            pl.BlockSpec((rows, BLOCK), lambda j: (0, first + j)),
        ],
        out_specs=pl.BlockSpec((rows, BLOCK), lambda j: (0, j)),
        compiler_params=params(),
        cost_estimate=cost(2 * rows * width * PIECE, 2 * width * PIECE, rows * PIECE),
    )(lengths, section, scales, xn, full, keys, values, x)


def stream_layer(full, buf, sems, xn_ref, q_ref, k_ref, v_ref, x_ref, lengths_ref, scale_ref, out_ref):
    blocks = x_ref.shape[1] // BLOCK

    def block(b):
        slot = lax.rem(b, SLOTS)
        at = pl.ds(pl.multiple_of(b * BLOCK, BLOCK), BLOCK)
        return pltpu.make_async_copy(full.at[:, at], buf.at[slot], sems.at[slot])

    def start():
        for b in range(SLOTS - 1):
            block(jnp.int32(b)).start()

    def run():
        q_ref[...] = jnp.zeros_like(q_ref)

        def emit(b):
            columns = pl.ds(pl.multiple_of(b * BLOCK, BLOCK), BLOCK)
            out_ref[:, columns] = attend(
                q_ref[...], k_ref, v_ref, x_ref[:, columns], lengths_ref, scale_ref[1], scale_ref[2]
            )

        def step(b, carry):
            slot = lax.rem(b, SLOTS)
            block(b).wait()

            @pl.when(b + SLOTS - 1 < blocks)
            def _():
                block(b + SLOTS - 1).start()

            acc = dot(xn_ref[...], buf[slot])
            emit(jnp.maximum(b - 1, 0))
            q_ref[...] = (acc * scale_ref[0]).astype(BF16)
            return carry

        lax.fori_loop(0, blocks, step, 0)
        emit(jnp.int32(blocks - 1))

    return start, run


def bring(pieces, out_ref, sems):
    at = 0
    copies = []
    for i, piece in enumerate(pieces):
        copies.append(pltpu.make_async_copy(piece, out_ref.at[:, pl.ds(at, piece.shape[1])], sems.at[i]))
        at += piece.shape[1]
    return copies


def encoder_kernel(count, *refs):
    section_ref, order_ref, lengths_ref, scale_ref, gain_ref, full = refs[:6]
    kv_refs, pieces = refs[6:8], refs[8 : 8 + count]
    out_ref, cross_ref = refs[8 + count : 10 + count]
    buf, sems, xn_ref, q_ref, x_ref, x_sems, kv_buf, kv_sems, k_ref, v_ref = refs[10 + count :]
    width = x_ref.shape[1]

    @pl.when(section_ref[0] == 1)
    def _():
        arrive = bring(pieces, x_ref, x_sems)
        for copy in arrive:
            copy.start()
        of_layer = lambda i: pltpu.make_async_copy(
            full.at[:, pl.ds(width, 2 * HEAD)], kv_buf.at[i], kv_sems.at[i]
        )

        def begin_later():
            for k in range(32):
                ref, row = kv_refs[k // 16], k % 16 * 128
                rows = pl.ds(pl.multiple_of(order_ref[k] * 128, 128), 128)
                for i in (1, 2):
                    block = ref.at[pl.ds(row, 128), pl.ds((i - 1) * 2 * HEAD, 2 * HEAD)]
                    pltpu.make_async_copy(block, kv_buf.at[i, rows], kv_sems.at[i]).start()

        of_layer(0).start()
        start, run = stream_layer(
            full, buf, sems, xn_ref, q_ref, k_ref, v_ref, x_ref, lengths_ref, scale_ref, out_ref
        )
        start()
        begin_later()
        for copy in arrive:
            copy.wait()
        norm_into(xn_ref, x_ref, gain_ref, 0)
        of_layer(0).wait()
        project_into(k_ref, v_ref, xn_ref[...], kv_buf[0])
        run()
        inv = inverse_norm(out_ref[...].astype(F32))
        for i in (1, 2):
            of_layer(i).wait()
        for i in (1, 2):
            xn_ref[...] = (out_ref[...].astype(F32) * inv * gain_ref[i : i + 1, :]).astype(BF16)
            at = (i - 1) * 2 * HEAD
            project_into(
                cross_ref.at[:, pl.ds(at, HEAD)],
                cross_ref.at[:, pl.ds(at + HEAD, HEAD)],
                xn_ref[...],
                kv_buf[i],
            )


def decoder_kernel(count, *refs):
    section_ref, lengths_ref, scale_ref, gain_ref, full, cross2_ref, cross3_ref, first_out, target = refs[:9]
    made, passed = refs[9 : 9 + count], refs[9 + count : 9 + 2 * count]
    out_ref = refs[9 + 2 * count]
    buf, sems, xn_ref, q_ref, x_ref, x_sems, mid_ref = refs[10 + 2 * count :]
    section = section_ref[0]
    blocks = x_ref.shape[1] // BLOCK
    cols = lambda ref, i: ref.at[:, pl.ds(i * HEAD, HEAD)]

    def fetch(pieces, into):
        copies = bring(pieces, into, x_sems)
        for copy in copies:
            copy.start()
        for copy in copies:
            copy.wait()

    def attend_all(cross_ref, into):
        def step(b, carry):
            columns = pl.ds(pl.multiple_of(b * BLOCK, BLOCK), BLOCK)
            into[:, columns] = attend(
                x_ref[:, columns], cols(cross_ref, 0), cols(cross_ref, 1), target[:, columns], lengths_ref, scale_ref[4], scale_ref[5]
            )
            return carry

        lax.fori_loop(0, blocks, step, 0)

    @pl.when(section == 0)
    def _():
        fetch(made, out_ref)

    @pl.when(section == 1)
    def _():
        fetch([first_out], out_ref)

    @pl.when(section == 2)
    def _():
        fetch(made, x_ref)
        attend_all(cross2_ref, out_ref)

    @pl.when(section == 3)
    def _():
        start, run = stream_layer(
            full, buf, sems, xn_ref, q_ref, cols(cross3_ref, 2), cols(cross3_ref, 3), mid_ref, lengths_ref, scale_ref, out_ref
        )
        copies = bring(passed, x_ref, x_sems)
        for copy in copies:
            copy.start()
        start()
        for copy in copies:
            copy.wait()
        attend_all(cross3_ref, mid_ref)
        norm_into(xn_ref, mid_ref, gain_ref, 0)
        run()


def unit_direction(along):
    return (along * lax.rsqrt(jnp.sum(along * along) + EPS)).astype(BF16)


def spectral_along(weight, kv_part, start_rows):
    of_kv = dot(start_rows, kv_part)
    parts = jnp.concatenate([dot(start_rows[0:1], weight)[0], of_kv[1, :HEAD], of_kv[2, HEAD:]])
    return total(parts.reshape(-1, 128))


def spectral_images(weight, kv_part, along):
    width = weight.shape[1]
    return jnp.stack(
        [
            dot(weight, unit_direction(along[:width])),
            dot(kv_part[:, :HEAD], unit_direction(along[width : width + HEAD])),
            dot(kv_part[:, HEAD:], unit_direction(along[width + HEAD :])),
        ]
    )


def shards(weights, kv_weights, gammas, gains, starts, source, target, lengths):
    weight, kv_part, gamma, gain, start_rows = weights[0], kv_weights[0], gammas[0], gains[0], starts[0]
    width = weight.shape[1]
    section = lax.axis_index("section").astype(jnp.int32).reshape(1)
    micro, seqs, length, _ = source.shape
    rows = micro * seqs * length
    seq_lengths = lengths.reshape(-1)
    source2 = source.reshape(rows, width)
    target2 = target.reshape(rows, width)
    wide_gain = gain.astype(F32).reshape(1, width)
    row_shape = jax.ShapeDtypeStruct((rows, width), BF16)
    head_shape = jax.ShapeDtypeStruct((rows, HEAD), BF16)

    hop = lambda value, pairs: lax.ppermute(value, "section", pairs)

    extra = jnp.concatenate([kv_part, gain.reshape(-1, 2 * HEAD)], 0)
    extra2 = hop(extra, [(2, 1)])
    extra3 = hop(extra, [(3, 1)])
    local = kv_part.shape[0]

    line = stack(ring(jnp.concatenate([extra2[:local], extra3[:local]], 1), along_first))
    kv_own = stack(ring(line, along_second))
    kv_other = send_one(kv_own, CORE_SWAP)
    full = lax.all_gather(jnp.concatenate([weight, kv_part], 1), "fsdp", axis=0, tiled=True)

    along = spectral_along(weight, kv_part, start_rows).reshape(-1)
    images = spectral_images(weight, kv_part, along)
    squares = jnp.broadcast_to(jnp.sum(images * images, axis=1)[:, None], (3, 128))
    sigmas = jnp.sqrt(total(squares)[:, 0] + EPS)
    scales, next_part = gamma / sigmas, images / sigmas[:, None]
    scales2 = hop(jnp.broadcast_to(scales[:, None], (3, 128)), [(2, 3)])[:, 0]

    x0, xn0 = pl.pallas_call(
        enter_kernel,
        out_shape=(row_shape, row_shape),
        in_specs=[SMEM, VMEM, VMEM, VMEM],
        out_specs=(VMEM, VMEM),
        compiler_params=params(),
        cost_estimate=cost(8 * rows * width, 8 * rows * width),
    )(section, source2, target2, wide_gain)

    kv_block = pl.BlockSpec((width, 2 * HEAD), lambda j: (0, width // (2 * HEAD)))
    whole = lambda shape: pl.BlockSpec(shape, lambda j: (0, 0))
    keys, values = pl.pallas_call(
        project_kernel,
        grid=(1,),
        out_shape=(head_shape, head_shape),
        in_specs=[whole((rows, width)), kv_block, ANY, ANY],
        out_specs=(whole((rows, HEAD)), whole((rows, HEAD))),
        compiler_params=params(),
        cost_estimate=cost(4 * rows * width * HEAD, 4 * width * HEAD),
    )(xn0, full, kv_own, kv_other)

    made, passed = [], []
    for at in range(0, width, PIECE):
        made.append(layer_part(xn0, full, keys, values, x0, at, seq_lengths, section, scales))
        passed.append(hop(made[-1], [(0, 1), (2, 3)]))

    scratch = [
        pltpu.VMEM((SLOTS, width, BLOCK), BF16),
        pltpu.SemaphoreType.DMA((SLOTS,)),
        pltpu.VMEM((rows, width), BF16),
        pltpu.VMEM((rows, BLOCK), BF16),
        pltpu.VMEM((rows, width), BF16),
        pltpu.SemaphoreType.DMA((len(made),)),
    ]
    n = len(made)
    all_gains = jnp.stack([gain, extra2[local:].reshape(-1), extra3[local:].reshape(-1)]).astype(F32)
    all_scales = jnp.concatenate([scales, jnp.where(section == 3, scales2, scales)])
    layer_cost = cost(2 * rows * width * width, 2 * width * width, rows * width)
    out1, cross = pl.pallas_call(
        functools.partial(encoder_kernel, n),
        out_shape=(row_shape, jax.ShapeDtypeStruct((rows, 4 * HEAD), BF16)),
        in_specs=[SMEM] * 4 + [VMEM] + [ANY] * (3 + n),
        out_specs=(VMEM, VMEM),
        scratch_shapes=scratch
        + [
            pltpu.VMEM((3, width, 2 * HEAD), BF16),
            pltpu.SemaphoreType.DMA((3,)),
            pltpu.VMEM((rows, HEAD), BF16),
            pltpu.VMEM((rows, HEAD), BF16),
        ],
        compiler_params=params(),
        cost_estimate=layer_cost,
    )(section, row_order(), seq_lengths, scales, all_gains, full, kv_own, kv_other, *passed)
    cross2, cross3 = hop(cross[:, : 2 * HEAD], [(1, 2)]), hop(cross, [(1, 3)])

    result = pl.pallas_call(
        functools.partial(decoder_kernel, n),
        out_shape=row_shape,
        in_specs=[SMEM] * 3 + [VMEM, ANY, VMEM, VMEM, ANY, VMEM] + [ANY] * (2 * n),
        out_specs=VMEM,
        scratch_shapes=scratch + [pltpu.VMEM((rows, width), BF16)],
        compiler_params=params(),
        cost_estimate=layer_cost,
    )(section, seq_lengths, all_scales, wide_gain, full, cross2, cross3, out1, target2, *made, *passed)
    return result.reshape(1, micro, seqs, length, width), next_part[None]


def solution(mesh):
    in_specs = (
        P("section", "fsdp", None),
        P("section", "fsdp", None),
        P("section", None),
        P("section", None),
        P("section", None, "fsdp"),
        P(None, "fsdp", None, None),
        P(None, "fsdp", None, None),
        P(None, "fsdp"),
    )
    out_specs = (P("section", None, "fsdp", None, None), P("section", None, "fsdp"))
    return jax.shard_map(shards, mesh=mesh, in_specs=in_specs, out_specs=out_specs, check_vma=False)
```

```python
import functools
import math

import jax
import jax.numpy as jnp
from jax import lax
from jax.experimental import pallas as pl
from jax.experimental.pallas import tpu as pltpu
from jax.sharding import PartitionSpec as P

HEAD = 128
EPS = 1e-06
F32 = jnp.float32
BF16 = jnp.bfloat16
VMEM_LIMIT = 48 * 1024 * 1024
BLOCK = 512
PIECES = (512, 512, 1024, 1024, 1024)
SLOTS = 3
LOG2E_SCALED = math.log2(math.e) / math.sqrt(HEAD)
ANY = pl.BlockSpec(memory_space=pl.ANY)
VMEM = pl.BlockSpec(memory_space=pltpu.VMEM)
SMEM = pl.BlockSpec(memory_space=pltpu.SMEM)


def dot(a, b):
    return jnp.dot(a, b, preferred_element_type=F32)


def moves(fn):
    pairs = []
    for index in range(32):
        x, z, core = index // 8, (index // 2) % 4, index % 2
        x2, z2, core2 = fn(x, z, core)
        pairs.append((index, (x2 % 4) * 8 + (z2 % 4) * 2 + core2))
    return pairs


ROUTE = (0, -1, 1, 2)
CORE_SWAP = moves(lambda x, z, c: (x, z, 1 - c))
DOUBLING = (
    CORE_SWAP,
    moves(lambda x, z, c: (x, z ^ 1, c)),
    moves(lambda x, z, c: (x ^ 1, z, c)),
    moves(lambda x, z, c: (x, z ^ 2, c)),
    moves(lambda x, z, c: (x ^ 2, z, c)),
)


def send(value, pairs):
    return lax.ppermute(value, "fsdp", pairs)


def along_first(step):
    return moves(lambda x, z, c: (x, z + step, c) if c == 0 else (x + step, z, c))


def along_second(step):
    return moves(lambda x, z, c: (x + step, z, c) if c == 0 else (x, z + step, c))


def send_one(value, pairs):
    return lax.ppermute(value, ("section", "fsdp"), [(32 + a, 32 + b) for a, b in pairs])


def ring(block, move):
    before, after = send_one(block, move(1)), send_one(block, move(-1))
    return [block, before, after, send_one(before, move(1))]


def row_order():
    index = lax.axis_index("fsdp")
    x, z, core = index // 8, (index // 2) % 4, index % 2
    first = jnp.array(ROUTE, jnp.int32)
    line, plane = jnp.tile(first, 4), jnp.repeat(first, 4)

    def order(kind):
        zs = z + jnp.where(kind == 0, line, plane)
        xs = x + jnp.where(kind == 0, plane, line)
        return ((xs + 8) % 4) * 8 + ((zs + 8) % 4) * 2 + kind

    return jnp.concatenate([order(core), order(1 - core)]).astype(jnp.int32)


def total(value):
    for pairs in DOUBLING:
        value = value + send(value, pairs)
    return value


def params():
    return pltpu.CompilerParams(vmem_limit_bytes=VMEM_LIMIT)


def cost(flops, size, exps=0):
    share = 64
    return pl.CostEstimate(flops=int(flops) // share, bytes_accessed=int(size) // share, transcendentals=int(exps) // share)


def stack_kernel(count, *refs):
    sources, out, held, sems = refs[:count], refs[count], refs[count + 1], refs[count + 2]
    rows = sources[0].shape[0]
    reads = [pltpu.make_async_copy(source, held.at[i], sems.at[0, i]) for i, source in enumerate(sources)]
    writes = [
        pltpu.make_async_copy(held.at[i], out.at[pl.ds(i * rows, rows)], sems.at[1, i]) for i in range(count)
    ]
    for read in reads:
        read.start()
    for read, write in zip(reads, writes):
        read.wait()
        write.start()
    for write in writes:
        write.wait()


def stack(blocks):
    count = len(blocks)
    rows, width = blocks[0].shape
    return pl.pallas_call(
        functools.partial(stack_kernel, count),
        out_shape=jax.ShapeDtypeStruct((count * rows, width), blocks[0].dtype),
        in_specs=[ANY] * count,
        out_specs=ANY,
        scratch_shapes=[pltpu.VMEM((count, rows, width), blocks[0].dtype), pltpu.SemaphoreType.DMA((2, count))],
        compiler_params=pltpu.CompilerParams(vmem_limit_bytes=12 * 1024 * 1024),
        cost_estimate=cost(0, 4 * count * rows * width),
    )(*blocks)


def copy_kernel(x_ref, *refs):
    refs[-1][...] = x_ref[...]


def copied(x, late):
    return pl.pallas_call(
        copy_kernel,
        out_shape=jax.ShapeDtypeStruct(x.shape, x.dtype),
        in_specs=[VMEM, ANY],
        out_specs=VMEM,
        compiler_params=params(),
        cost_estimate=cost(0, 0),
    )(x, late)


def inverse_norm(wide):
    return lax.rsqrt(jnp.mean(wide * wide, axis=-1, keepdims=True) + EPS)


def norm_into(xn_ref, x_ref, gain_ref, row):
    wide = x_ref[...].astype(F32)
    xn_ref[...] = (wide * inverse_norm(wide) * gain_ref[row : row + 1, :]).astype(BF16)


def attend(q, keys_ref, values_ref, resid, lengths_ref, key_scale, value_scale):
    seqs, heads = q.shape[0] // 128, q.shape[1] // HEAD
    position = lax.broadcasted_iota(jnp.int32, (heads * 128, 128), 1)
    made = []
    for m in range(seqs):
        rows = slice(m * 128, (m + 1) * 128)
        stacked = jnp.concatenate([q[rows, h * HEAD : (h + 1) * HEAD] for h in range(heads)], 0)
        scores = lax.dot_general(
            stacked, keys_ref[rows, :], (((1,), (1,)), ((), ())), preferred_element_type=F32
        )
        expd = jnp.where(position < lengths_ref[m], jnp.exp2(scores * (key_scale * LOG2E_SCALED)), 0.0)
        probs = (expd * (1.0 / jnp.sum(expd, axis=-1, keepdims=True))).astype(BF16)
        context = dot(probs, values_ref[rows, :]) * value_scale
        made.append(jnp.concatenate([context[h * 128 : (h + 1) * 128] for h in range(heads)], 1))
    return (resid.astype(F32) + jnp.concatenate(made, 0)).astype(BF16)


def project_into(keys_ref, values_ref, xn, kv):
    projected = dot(xn, kv).astype(BF16)
    keys_ref[...] = projected[:, :HEAD]
    values_ref[...] = projected[:, HEAD:]


def enter_kernel(section_ref, source_ref, target_ref, gain_ref, x_ref, xn_ref):
    @pl.when(section_ref[0] == 2)
    def _():
        x_ref[...] = target_ref[...]

    @pl.when(section_ref[0] != 2)
    def _():
        x_ref[...] = source_ref[...]

    norm_into(xn_ref, x_ref, gain_ref, 0)


def project_kernel(xn_ref, kv_ref, *refs):
    keys_ref, values_ref = refs[-2:]
    project_into(keys_ref, values_ref, xn_ref[...], kv_ref[...])


def part_kernel(lengths_ref, section_ref, scale_ref, xn_ref, w_ref, k_ref, v_ref, x_ref, out_ref):
    query = lambda: (dot(xn_ref[...], w_ref[...]) * scale_ref[0]).astype(BF16)

    @pl.when(section_ref[0] == 0)
    def _():
        out_ref[...] = attend(query(), k_ref, v_ref, x_ref[...], lengths_ref, scale_ref[1], scale_ref[2])

    @pl.when(section_ref[0] == 2)
    def _():
        out_ref[...] = query()

    @pl.when(lax.rem(section_ref[0], 2) == 1)
    def _():
        out_ref[...] = jnp.zeros_like(out_ref)


def layer_part(xn, full, keys, values, x, at, piece, lengths, section, scales):
    rows, width = xn.shape
    first = at // BLOCK
    whole = lambda a: pl.BlockSpec(a.shape, lambda j: (0, 0))
    return pl.pallas_call(
        part_kernel,
        grid=(piece // BLOCK,),
        out_shape=jax.ShapeDtypeStruct((rows, piece), BF16),
        in_specs=[
            SMEM,
            SMEM,
            SMEM,
            whole(xn),
            pl.BlockSpec((width, BLOCK), lambda j: (0, first + j)),
            whole(keys),
            whole(values),
            pl.BlockSpec((rows, BLOCK), lambda j: (0, first + j)),
        ],
        out_specs=pl.BlockSpec((rows, BLOCK), lambda j: (0, j)),
        compiler_params=params(),
        cost_estimate=cost(2 * rows * width * piece, 2 * width * piece, rows * piece),
    )(lengths, section, scales, xn, full, keys, values, x)


def stream_layer(full, buf, sems, xn_ref, q_ref, k_ref, v_ref, x_ref, lengths_ref, scale_ref, out_ref):
    blocks = x_ref.shape[1] // BLOCK

    def block(b):
        slot = lax.rem(b, SLOTS)
        at = pl.ds(pl.multiple_of(b * BLOCK, BLOCK), BLOCK)
        return pltpu.make_async_copy(full.at[:, at], buf.at[slot], sems.at[slot])

    def start():
        for b in range(SLOTS - 1):
            block(jnp.int32(b)).start()

    def run():
        q_ref[...] = jnp.zeros_like(q_ref)

        def emit(b):
            columns = pl.ds(pl.multiple_of(b * BLOCK, BLOCK), BLOCK)
            out_ref[:, columns] = attend(
                q_ref[...], k_ref, v_ref, x_ref[:, columns], lengths_ref, scale_ref[1], scale_ref[2]
            )

        def step(b, carry):
            slot = lax.rem(b, SLOTS)
            block(b).wait()

            @pl.when(b + SLOTS - 1 < blocks)
            def _():
                block(b + SLOTS - 1).start()

            acc = dot(xn_ref[...], buf[slot])
            emit(jnp.maximum(b - 1, 0))
            q_ref[...] = (acc * scale_ref[0]).astype(BF16)
            return carry

        lax.fori_loop(0, blocks, step, 0)
        emit(jnp.int32(blocks - 1))

    return start, run


def bring(pieces, out_ref, sems):
    at = 0
    copies = []
    for i, piece in enumerate(pieces):
        copies.append(pltpu.make_async_copy(piece, out_ref.at[:, pl.ds(at, piece.shape[1])], sems.at[i]))
        at += piece.shape[1]
    return copies


def encoder_kernel(count, *refs):
    section_ref, order_ref, lengths_ref, scale_ref, gain_ref, full = refs[:6]
    kv_refs, pieces = refs[6:8], refs[8 : 8 + count]
    out_ref, cross_ref = refs[8 + count : 10 + count]
    buf, sems, xn_ref, q_ref, x_ref, x_sems, kv_buf, kv_sems, k_ref, v_ref = refs[10 + count :]
    width = x_ref.shape[1]

    @pl.when(section_ref[0] == 1)
    def _():
        arrive = bring(pieces, x_ref, x_sems)
        for copy in arrive:
            copy.start()
        of_layer = lambda i: pltpu.make_async_copy(
            full.at[:, pl.ds(width, 2 * HEAD)], kv_buf.at[i], kv_sems.at[i]
        )

        def begin_later():
            for k in range(32):
                ref, row = kv_refs[k // 16], k % 16 * 128
                rows = pl.ds(pl.multiple_of(order_ref[k] * 128, 128), 128)
                for i in (1, 2):
                    block = ref.at[pl.ds(row, 128), pl.ds((i - 1) * 2 * HEAD, 2 * HEAD)]
                    pltpu.make_async_copy(block, kv_buf.at[i, rows], kv_sems.at[i]).start()

        of_layer(0).start()
        start, run = stream_layer(
            full, buf, sems, xn_ref, q_ref, k_ref, v_ref, x_ref, lengths_ref, scale_ref, out_ref
        )
        start()
        begin_later()
        for copy in arrive:
            copy.wait()
        norm_into(xn_ref, x_ref, gain_ref, 0)
        of_layer(0).wait()
        project_into(k_ref, v_ref, xn_ref[...], kv_buf[0])
        run()
        inv = inverse_norm(out_ref[...].astype(F32))
        for i in (1, 2):
            of_layer(i).wait()
        for i in (1, 2):
            xn_ref[...] = (out_ref[...].astype(F32) * inv * gain_ref[i : i + 1, :]).astype(BF16)
            at = (i - 1) * 2 * HEAD
            project_into(
                cross_ref.at[:, pl.ds(at, HEAD)],
                cross_ref.at[:, pl.ds(at + HEAD, HEAD)],
                xn_ref[...],
                kv_buf[i],
            )


def decoder_kernel(count, *refs):
    section_ref, lengths_ref, scale_ref, gain_ref, full, cross2_ref, cross3_ref, first_out, target = refs[:9]
    made, passed = refs[9 : 9 + count], refs[9 + count : 9 + 2 * count]
    out_ref = refs[9 + 2 * count]
    buf, sems, xn_ref, q_ref, x_ref, x_sems, mid_ref = refs[10 + 2 * count :]
    section = section_ref[0]
    blocks = x_ref.shape[1] // BLOCK
    cols = lambda ref, i: ref.at[:, pl.ds(i * HEAD, HEAD)]

    def fetch(pieces, into):
        copies = bring(pieces, into, x_sems)
        for copy in copies:
            copy.start()
        for copy in copies:
            copy.wait()

    def attend_all(cross_ref, into):
        def step(b, carry):
            columns = pl.ds(pl.multiple_of(b * BLOCK, BLOCK), BLOCK)
            into[:, columns] = attend(
                x_ref[:, columns], cols(cross_ref, 0), cols(cross_ref, 1), target[:, columns], lengths_ref, scale_ref[4], scale_ref[5]
            )
            return carry

        lax.fori_loop(0, blocks, step, 0)

    @pl.when(section == 0)
    def _():
        fetch(made, out_ref)

    @pl.when(section == 1)
    def _():
        fetch([first_out], out_ref)

    @pl.when(section == 2)
    def _():
        fetch(made, x_ref)
        attend_all(cross2_ref, out_ref)

    @pl.when(section == 3)
    def _():
        start, run = stream_layer(
            full, buf, sems, xn_ref, q_ref, cols(cross3_ref, 2), cols(cross3_ref, 3), mid_ref, lengths_ref, scale_ref, out_ref
        )
        copies = bring(passed, x_ref, x_sems)
        for copy in copies:
            copy.start()
        start()
        for copy in copies:
            copy.wait()
        attend_all(cross3_ref, mid_ref)
        norm_into(xn_ref, mid_ref, gain_ref, 0)
        run()


def unit_direction(along):
    return (along * lax.rsqrt(jnp.sum(along * along) + EPS)).astype(BF16)


def spectral_along(weight, kv_part, start_rows):
    of_kv = dot(start_rows, kv_part)
    parts = jnp.concatenate([dot(start_rows[0:1], weight)[0], of_kv[1, :HEAD], of_kv[2, HEAD:]])
    return total(parts.reshape(-1, 128))


def spectral_images(weight, kv_part, along):
    width = weight.shape[1]
    return jnp.stack(
        [
            dot(weight, unit_direction(along[:width])),
            dot(kv_part[:, :HEAD], unit_direction(along[width : width + HEAD])),
            dot(kv_part[:, HEAD:], unit_direction(along[width + HEAD :])),
        ]
    )


def shards(weights, kv_weights, gammas, gains, starts, source, target, lengths):
    weight, kv_part, gamma, gain, start_rows = weights[0], kv_weights[0], gammas[0], gains[0], starts[0]
    width = weight.shape[1]
    section = lax.axis_index("section").astype(jnp.int32).reshape(1)
    micro, seqs, length, _ = source.shape
    rows = micro * seqs * length
    seq_lengths = lengths.reshape(-1)
    source2 = source.reshape(rows, width)
    target2 = target.reshape(rows, width)
    wide_gain = gain.astype(F32).reshape(1, width)
    row_shape = jax.ShapeDtypeStruct((rows, width), BF16)
    head_shape = jax.ShapeDtypeStruct((rows, HEAD), BF16)

    hop = lambda value, pairs: lax.ppermute(value, "section", pairs)

    extra = jnp.concatenate([kv_part, gain.reshape(-1, 2 * HEAD)], 0)
    extra2 = hop(extra, [(2, 1)])
    extra3 = hop(extra, [(3, 1)])
    local = kv_part.shape[0]

    line = stack(ring(jnp.concatenate([extra2[:local], extra3[:local]], 1), along_first))
    kv_own = stack(ring(line, along_second))
    kv_other = send_one(kv_own, CORE_SWAP)
    full = lax.all_gather(jnp.concatenate([weight, kv_part], 1), "fsdp", axis=0, tiled=True)

    along = spectral_along(weight, kv_part, start_rows).reshape(-1)
    images = spectral_images(weight, kv_part, along)
    squares = jnp.broadcast_to(jnp.sum(images * images, axis=1)[:, None], (3, 128))
    sigmas = jnp.sqrt(total(squares)[:, 0] + EPS)
    scales, next_part = gamma / sigmas, images / sigmas[:, None]
    scales2 = hop(jnp.broadcast_to(scales[:, None], (3, 128)), [(2, 3)])[:, 0]

    x0, xn0 = pl.pallas_call(
        enter_kernel,
        out_shape=(row_shape, row_shape),
        in_specs=[SMEM, VMEM, VMEM, VMEM],
        out_specs=(VMEM, VMEM),
        compiler_params=params(),
        cost_estimate=cost(8 * rows * width, 8 * rows * width),
    )(section, source2, target2, wide_gain)

    kv_block = pl.BlockSpec((width, 2 * HEAD), lambda j: (0, width // (2 * HEAD)))
    whole = lambda shape: pl.BlockSpec(shape, lambda j: (0, 0))
    keys, values = pl.pallas_call(
        project_kernel,
        grid=(1,),
        out_shape=(head_shape, head_shape),
        in_specs=[whole((rows, width)), kv_block, ANY, ANY],
        out_specs=(whole((rows, HEAD)), whole((rows, HEAD))),
        compiler_params=params(),
        cost_estimate=cost(4 * rows * width * HEAD, 4 * width * HEAD),
    )(xn0, full, kv_own, kv_other)

    made, passed = [], []
    at = 0
    for i, piece in enumerate(PIECES):
        made.append(layer_part(xn0, full, keys, values, x0, at, piece, seq_lengths, section, scales))
        at += piece
        if i == 0:
            relay = hop(made[0], [(0, 3), (2, 1)])
        else:
            passed.append(hop(made[-1], [(0, 1), (2, 3)]))
        if i == 2:
            relay = hop(copied(relay, made[-1]), [(3, 2), (1, 0)])
        if i == 3:
            relay = hop(copied(relay, made[-1]), [(2, 1), (0, 3)])
    passed = [relay] + passed

    scratch = [
        pltpu.VMEM((SLOTS, width, BLOCK), BF16),
        pltpu.SemaphoreType.DMA((SLOTS,)),
        pltpu.VMEM((rows, width), BF16),
        pltpu.VMEM((rows, BLOCK), BF16),
        pltpu.VMEM((rows, width), BF16),
        pltpu.SemaphoreType.DMA((len(made),)),
    ]
    n = len(made)
    all_gains = jnp.stack([gain, extra2[local:].reshape(-1), extra3[local:].reshape(-1)]).astype(F32)
    all_scales = jnp.concatenate([scales, jnp.where(section == 3, scales2, scales)])
    layer_cost = cost(2 * rows * width * width, 2 * width * width, rows * width)
    out1, cross = pl.pallas_call(
        functools.partial(encoder_kernel, n),
        out_shape=(row_shape, jax.ShapeDtypeStruct((rows, 4 * HEAD), BF16)),
        in_specs=[SMEM] * 4 + [VMEM] + [ANY] * (3 + n),
        out_specs=(VMEM, VMEM),
        scratch_shapes=scratch
        + [
            pltpu.VMEM((3, width, 2 * HEAD), BF16),
            pltpu.SemaphoreType.DMA((3,)),
            pltpu.VMEM((rows, HEAD), BF16),
            pltpu.VMEM((rows, HEAD), BF16),
        ],
        compiler_params=params(),
        cost_estimate=layer_cost,
    )(section, row_order(), seq_lengths, scales, all_gains, full, kv_own, kv_other, *passed)
    cross2, cross3 = hop(cross[:, : 2 * HEAD], [(1, 2)]), hop(cross, [(1, 3)])

    result = pl.pallas_call(
        functools.partial(decoder_kernel, n),
        out_shape=row_shape,
        in_specs=[SMEM] * 3 + [VMEM, ANY, VMEM, VMEM, ANY, VMEM] + [ANY] * (2 * n),
        out_specs=VMEM,
        scratch_shapes=scratch + [pltpu.VMEM((rows, width), BF16)],
        compiler_params=params(),
        cost_estimate=layer_cost,
    )(section, seq_lengths, all_scales, wide_gain, full, cross2, cross3, out1, target2, *made, *passed)
    return result.reshape(1, micro, seqs, length, width), next_part[None]


def solution(mesh):
    in_specs = (
        P("section", "fsdp", None),
        P("section", "fsdp", None),
        P("section", None),
        P("section", None),
        P("section", None, "fsdp"),
        P(None, "fsdp", None, None),
        P(None, "fsdp", None, None),
        P(None, "fsdp"),
    )
    out_specs = (P("section", None, "fsdp", None, None), P("section", None, "fsdp"))
    return jax.shard_map(shards, mesh=mesh, in_specs=in_specs, out_specs=out_specs, check_vma=False)
```

```python
import functools
import math

import jax
import jax.numpy as jnp
from jax import lax
from jax.experimental import pallas as pl
from jax.experimental.pallas import tpu as pltpu
from jax.sharding import PartitionSpec as P

HEAD = 128
EPS = 1e-06
F32 = jnp.float32
BF16 = jnp.bfloat16
VMEM_LIMIT = 48 * 1024 * 1024
BLOCK = 512
PIECES = (512,) * 8
SLOTS = 3
LOG2E_SCALED = math.log2(math.e) / math.sqrt(HEAD)
ANY = pl.BlockSpec(memory_space=pl.ANY)
VMEM = pl.BlockSpec(memory_space=pltpu.VMEM)
SMEM = pl.BlockSpec(memory_space=pltpu.SMEM)


def dot(a, b):
    return jnp.dot(a, b, preferred_element_type=F32)


def moves(fn):
    pairs = []
    for index in range(32):
        x, z, core = index // 8, (index // 2) % 4, index % 2
        x2, z2, core2 = fn(x, z, core)
        pairs.append((index, (x2 % 4) * 8 + (z2 % 4) * 2 + core2))
    return pairs


ROUTE = (0, -1, 1, 2)
CORE_SWAP = moves(lambda x, z, c: (x, z, 1 - c))
DOUBLING = (
    CORE_SWAP,
    moves(lambda x, z, c: (x, z ^ 1, c)),
    moves(lambda x, z, c: (x ^ 1, z, c)),
    moves(lambda x, z, c: (x, z ^ 2, c)),
    moves(lambda x, z, c: (x ^ 2, z, c)),
)


def send(value, pairs):
    return lax.ppermute(value, "fsdp", pairs)


def along_first(step):
    return moves(lambda x, z, c: (x, z + step, c) if c == 0 else (x + step, z, c))


def along_second(step):
    return moves(lambda x, z, c: (x + step, z, c) if c == 0 else (x, z + step, c))


def send_one(value, pairs):
    return lax.ppermute(value, ("section", "fsdp"), [(32 + a, 32 + b) for a, b in pairs])


def ring(block, move):
    before, after = send_one(block, move(1)), send_one(block, move(-1))
    return [block, before, after, send_one(before, move(1))]


def row_order():
    index = lax.axis_index("fsdp")
    x, z, core = index // 8, (index // 2) % 4, index % 2
    first = jnp.array(ROUTE, jnp.int32)
    line, plane = jnp.tile(first, 4), jnp.repeat(first, 4)

    def order(kind):
        zs = z + jnp.where(kind == 0, line, plane)
        xs = x + jnp.where(kind == 0, plane, line)
        return ((xs + 8) % 4) * 8 + ((zs + 8) % 4) * 2 + kind

    return jnp.concatenate([order(core), order(1 - core)]).astype(jnp.int32)


def total(value):
    for pairs in DOUBLING:
        value = value + send(value, pairs)
    return value


def params():
    return pltpu.CompilerParams(vmem_limit_bytes=VMEM_LIMIT)


def cost(flops, size, exps=0):
    share = 64
    return pl.CostEstimate(flops=int(flops) // share, bytes_accessed=int(size) // share, transcendentals=int(exps) // share)


def stack_kernel(count, *refs):
    sources, out, held, sems = refs[:count], refs[count], refs[count + 1], refs[count + 2]
    rows = sources[0].shape[0]
    reads = [pltpu.make_async_copy(source, held.at[i], sems.at[0, i]) for i, source in enumerate(sources)]
    writes = [
        pltpu.make_async_copy(held.at[i], out.at[pl.ds(i * rows, rows)], sems.at[1, i]) for i in range(count)
    ]
    for read in reads:
        read.start()
    for read, write in zip(reads, writes):
        read.wait()
        write.start()
    for write in writes:
        write.wait()


def stack(blocks):
    count = len(blocks)
    rows, width = blocks[0].shape
    return pl.pallas_call(
        functools.partial(stack_kernel, count),
        out_shape=jax.ShapeDtypeStruct((count * rows, width), blocks[0].dtype),
        in_specs=[ANY] * count,
        out_specs=ANY,
        scratch_shapes=[pltpu.VMEM((count, rows, width), blocks[0].dtype), pltpu.SemaphoreType.DMA((2, count))],
        compiler_params=pltpu.CompilerParams(vmem_limit_bytes=12 * 1024 * 1024),
        cost_estimate=cost(0, 4 * count * rows * width),
    )(*blocks)


def inverse_norm(wide):
    return lax.rsqrt(jnp.mean(wide * wide, axis=-1, keepdims=True) + EPS)


def norm_into(xn_ref, x_ref, gain_ref, row):
    wide = x_ref[...].astype(F32)
    xn_ref[...] = (wide * inverse_norm(wide) * gain_ref[row : row + 1, :]).astype(BF16)


def attend(q, keys_ref, values_ref, resid, lengths_ref, key_scale, value_scale):
    seqs, heads = q.shape[0] // 128, q.shape[1] // HEAD
    position = lax.broadcasted_iota(jnp.int32, (heads * 128, 128), 1)
    made = []
    for m in range(seqs):
        rows = slice(m * 128, (m + 1) * 128)
        stacked = jnp.concatenate([q[rows, h * HEAD : (h + 1) * HEAD] for h in range(heads)], 0)
        scores = lax.dot_general(
            stacked, keys_ref[rows, :], (((1,), (1,)), ((), ())), preferred_element_type=F32
        )
        expd = jnp.where(position < lengths_ref[m], jnp.exp2(scores * (key_scale * LOG2E_SCALED)), 0.0)
        probs = (expd * (1.0 / jnp.sum(expd, axis=-1, keepdims=True))).astype(BF16)
        context = dot(probs, values_ref[rows, :]) * value_scale
        made.append(jnp.concatenate([context[h * 128 : (h + 1) * 128] for h in range(heads)], 1))
    return (resid.astype(F32) + jnp.concatenate(made, 0)).astype(BF16)


def project_into(keys_ref, values_ref, xn, kv):
    projected = dot(xn, kv).astype(BF16)
    keys_ref[...] = projected[:, :HEAD]
    values_ref[...] = projected[:, HEAD:]


def enter_kernel(section_ref, source_ref, target_ref, gain_ref, x_ref, xn_ref):
    @pl.when(section_ref[0] == 2)
    def _():
        x_ref[...] = target_ref[...]

    @pl.when(section_ref[0] != 2)
    def _():
        x_ref[...] = source_ref[...]

    norm_into(xn_ref, x_ref, gain_ref, 0)


def project_kernel(xn_ref, kv_ref, *refs):
    keys_ref, values_ref = refs[-2:]
    project_into(keys_ref, values_ref, xn_ref[...], kv_ref[...])


def part_kernel(lengths_ref, section_ref, scale_ref, xn_ref, w_ref, k_ref, v_ref, x_ref, out_ref):
    query = lambda: (dot(xn_ref[...], w_ref[...]) * scale_ref[0]).astype(BF16)

    @pl.when(section_ref[0] == 0)
    def _():
        out_ref[...] = attend(query(), k_ref, v_ref, x_ref[...], lengths_ref, scale_ref[1], scale_ref[2])

    @pl.when(section_ref[0] == 2)
    def _():
        out_ref[...] = query()

    @pl.when(lax.rem(section_ref[0], 2) == 1)
    def _():
        out_ref[...] = jnp.zeros_like(out_ref)


def layer_part(xn, full, keys, values, x, at, piece, lengths, section, scales):
    rows, width = xn.shape
    first = at // BLOCK
    whole = lambda a: pl.BlockSpec(a.shape, lambda j: (0, 0))
    return pl.pallas_call(
        part_kernel,
        grid=(piece // BLOCK,),
        out_shape=jax.ShapeDtypeStruct((rows, piece), BF16),
        in_specs=[
            SMEM,
            SMEM,
            SMEM,
            whole(xn),
            pl.BlockSpec((width, BLOCK), lambda j: (0, first + j)),
            whole(keys),
            whole(values),
            pl.BlockSpec((rows, BLOCK), lambda j: (0, first + j)),
        ],
        out_specs=pl.BlockSpec((rows, BLOCK), lambda j: (0, j)),
        compiler_params=params(),
        cost_estimate=cost(2 * rows * width * piece, 2 * width * piece, rows * piece),
    )(lengths, section, scales, xn, full, keys, values, x)


def stream_layer(full, buf, sems, xn_ref, q_ref, k_ref, v_ref, x_ref, lengths_ref, scale_ref, out_ref):
    blocks = x_ref.shape[1] // BLOCK

    def block(b):
        slot = lax.rem(b, SLOTS)
        at = pl.ds(pl.multiple_of(b * BLOCK, BLOCK), BLOCK)
        return pltpu.make_async_copy(full.at[:, at], buf.at[slot], sems.at[slot])

    def start():
        for b in range(SLOTS - 1):
            block(jnp.int32(b)).start()

    def run():
        q_ref[...] = jnp.zeros_like(q_ref)

        def emit(b):
            columns = pl.ds(pl.multiple_of(b * BLOCK, BLOCK), BLOCK)
            out_ref[:, columns] = attend(
                q_ref[...], k_ref, v_ref, x_ref[:, columns], lengths_ref, scale_ref[1], scale_ref[2]
            )

        def step(b, carry):
            slot = lax.rem(b, SLOTS)
            block(b).wait()

            @pl.when(b + SLOTS - 1 < blocks)
            def _():
                block(b + SLOTS - 1).start()

            acc = dot(xn_ref[...], buf[slot])
            emit(jnp.maximum(b - 1, 0))
            q_ref[...] = (acc * scale_ref[0]).astype(BF16)
            return carry

        lax.fori_loop(0, blocks, step, 0)
        emit(jnp.int32(blocks - 1))

    return start, run


def bring(pieces, out_ref, sems):
    at = 0
    copies = []
    for i, piece in enumerate(pieces):
        copies.append(pltpu.make_async_copy(piece, out_ref.at[:, pl.ds(at, piece.shape[1])], sems.at[i]))
        at += piece.shape[1]
    return copies


def encoder_kernel(count, *refs):
    section_ref, order_ref, lengths_ref, scale_ref, gain_ref, full = refs[:6]
    kv_refs, pieces = refs[6:8], refs[8 : 8 + count]
    out_ref, cross_ref = refs[8 + count : 10 + count]
    buf, sems, xn_ref, q_ref, x_ref, x_sems, kv_buf, kv_sems, k_ref, v_ref = refs[10 + count :]
    width = x_ref.shape[1]

    @pl.when(section_ref[0] == 1)
    def _():
        arrive = bring(pieces, x_ref, x_sems)
        for copy in arrive:
            copy.start()
        of_layer = lambda i: pltpu.make_async_copy(
            full.at[:, pl.ds(width, 2 * HEAD)], kv_buf.at[i], kv_sems.at[i]
        )

        def begin_later():
            for k in range(32):
                ref, row = kv_refs[k // 16], k % 16 * 128
                rows = pl.ds(pl.multiple_of(order_ref[k] * 128, 128), 128)
                for i in (1, 2):
                    block = ref.at[pl.ds(row, 128), pl.ds((i - 1) * 2 * HEAD, 2 * HEAD)]
                    pltpu.make_async_copy(block, kv_buf.at[i, rows], kv_sems.at[i]).start()

        of_layer(0).start()
        start, run = stream_layer(
            full, buf, sems, xn_ref, q_ref, k_ref, v_ref, x_ref, lengths_ref, scale_ref, out_ref
        )
        start()
        begin_later()
        for copy in arrive:
            copy.wait()
        norm_into(xn_ref, x_ref, gain_ref, 0)
        of_layer(0).wait()
        project_into(k_ref, v_ref, xn_ref[...], kv_buf[0])
        run()
        inv = inverse_norm(out_ref[...].astype(F32))
        for i in (1, 2):
            of_layer(i).wait()
        for i in (1, 2):
            xn_ref[...] = (out_ref[...].astype(F32) * inv * gain_ref[i : i + 1, :]).astype(BF16)
            at = (i - 1) * 2 * HEAD
            project_into(
                cross_ref.at[:, pl.ds(at, HEAD)],
                cross_ref.at[:, pl.ds(at + HEAD, HEAD)],
                xn_ref[...],
                kv_buf[i],
            )


def decoder_kernel(count, *refs):
    section_ref, lengths_ref, scale_ref, gain_ref, full, cross2_ref, cross3_ref, first_out, target = refs[:9]
    made, passed = refs[9 : 9 + count], refs[9 + count : 9 + 2 * count]
    out_ref = refs[9 + 2 * count]
    buf, sems, xn_ref, q_ref, x_ref, x_sems, mid_ref = refs[10 + 2 * count :]
    section = section_ref[0]
    blocks = x_ref.shape[1] // BLOCK
    cols = lambda ref, i: ref.at[:, pl.ds(i * HEAD, HEAD)]

    def fetch(pieces, into):
        copies = bring(pieces, into, x_sems)
        for copy in copies:
            copy.start()
        for copy in copies:
            copy.wait()

    def attend_all(cross_ref, into):
        def step(b, carry):
            columns = pl.ds(pl.multiple_of(b * BLOCK, BLOCK), BLOCK)
            into[:, columns] = attend(
                x_ref[:, columns], cols(cross_ref, 0), cols(cross_ref, 1), target[:, columns], lengths_ref, scale_ref[4], scale_ref[5]
            )
            return carry

        lax.fori_loop(0, blocks, step, 0)

    @pl.when(section == 0)
    def _():
        fetch(made, out_ref)

    @pl.when(section == 1)
    def _():
        fetch([first_out], out_ref)

    @pl.when(section == 2)
    def _():
        fetch(made, x_ref)
        attend_all(cross2_ref, out_ref)

    @pl.when(section == 3)
    def _():
        start, run = stream_layer(
            full, buf, sems, xn_ref, q_ref, cols(cross3_ref, 2), cols(cross3_ref, 3), mid_ref, lengths_ref, scale_ref, out_ref
        )
        copies = bring(passed, x_ref, x_sems)
        for copy in copies:
            copy.start()
        start()
        for copy in copies:
            copy.wait()
        attend_all(cross3_ref, mid_ref)
        norm_into(xn_ref, mid_ref, gain_ref, 0)
        run()


def unit_direction(along):
    return (along * lax.rsqrt(jnp.sum(along * along) + EPS)).astype(BF16)


def spectral_along(weight, kv_part, start_rows):
    of_kv = dot(start_rows, kv_part)
    parts = jnp.concatenate([dot(start_rows[0:1], weight)[0], of_kv[1, :HEAD], of_kv[2, HEAD:]])
    return total(parts.reshape(-1, 128))


def spectral_images(weight, kv_part, along):
    width = weight.shape[1]
    return jnp.stack(
        [
            dot(weight, unit_direction(along[:width])),
            dot(kv_part[:, :HEAD], unit_direction(along[width : width + HEAD])),
            dot(kv_part[:, HEAD:], unit_direction(along[width + HEAD :])),
        ]
    )


def shards(weights, kv_weights, gammas, gains, starts, source, target, lengths):
    weight, kv_part, gamma, gain, start_rows = weights[0], kv_weights[0], gammas[0], gains[0], starts[0]
    width = weight.shape[1]
    section = lax.axis_index("section").astype(jnp.int32).reshape(1)
    micro, seqs, length, _ = source.shape
    rows = micro * seqs * length
    seq_lengths = lengths.reshape(-1)
    source2 = source.reshape(rows, width)
    target2 = target.reshape(rows, width)
    wide_gain = gain.astype(F32).reshape(1, width)
    row_shape = jax.ShapeDtypeStruct((rows, width), BF16)
    head_shape = jax.ShapeDtypeStruct((rows, HEAD), BF16)

    hop = lambda value, pairs: lax.ppermute(value, "section", pairs)

    extra = jnp.concatenate([kv_part, gain.reshape(-1, 2 * HEAD)], 0)
    extra2 = hop(extra, [(2, 1)])
    extra3 = hop(extra, [(3, 1)])
    local = kv_part.shape[0]

    line = stack(ring(jnp.concatenate([extra2[:local], extra3[:local]], 1), along_first))
    kv_own = stack(ring(line, along_second))
    kv_other = send_one(kv_own, CORE_SWAP)
    full = lax.all_gather(jnp.concatenate([weight, kv_part], 1), "fsdp", axis=0, tiled=True)

    along = spectral_along(weight, kv_part, start_rows).reshape(-1)
    images = spectral_images(weight, kv_part, along)
    squares = jnp.broadcast_to(jnp.sum(images * images, axis=1)[:, None], (3, 128))
    sigmas = jnp.sqrt(total(squares)[:, 0] + EPS)
    scales, next_part = gamma / sigmas, images / sigmas[:, None]
    scales2 = hop(jnp.broadcast_to(scales[:, None], (3, 128)), [(2, 3)])[:, 0]

    x0, xn0 = pl.pallas_call(
        enter_kernel,
        out_shape=(row_shape, row_shape),
        in_specs=[SMEM, VMEM, VMEM, VMEM],
        out_specs=(VMEM, VMEM),
        compiler_params=params(),
        cost_estimate=cost(8 * rows * width, 8 * rows * width),
    )(section, source2, target2, wide_gain)

    kv_block = pl.BlockSpec((width, 2 * HEAD), lambda j: (0, width // (2 * HEAD)))
    whole = lambda shape: pl.BlockSpec(shape, lambda j: (0, 0))
    keys, values = pl.pallas_call(
        project_kernel,
        grid=(1,),
        out_shape=(head_shape, head_shape),
        in_specs=[whole((rows, width)), kv_block, ANY, ANY],
        out_specs=(whole((rows, HEAD)), whole((rows, HEAD))),
        compiler_params=params(),
        cost_estimate=cost(4 * rows * width * HEAD, 4 * width * HEAD),
    )(xn0, full, kv_own, kv_other)

    made, passed = [], []
    at = 0
    for piece in PIECES:
        made.append(layer_part(xn0, full, keys, values, x0, at, piece, seq_lengths, section, scales))
        passed.append(hop(made[-1], [(0, 1), (2, 3)]))
        at += piece

    scratch = [
        pltpu.VMEM((SLOTS, width, BLOCK), BF16),
        pltpu.SemaphoreType.DMA((SLOTS,)),
        pltpu.VMEM((rows, width), BF16),
        pltpu.VMEM((rows, BLOCK), BF16),
        pltpu.VMEM((rows, width), BF16),
        pltpu.SemaphoreType.DMA((len(made),)),
    ]
    n = len(made)
    all_gains = jnp.stack([gain, extra2[local:].reshape(-1), extra3[local:].reshape(-1)]).astype(F32)
    all_scales = jnp.concatenate([scales, jnp.where(section == 3, scales2, scales)])
    layer_cost = cost(2 * rows * width * width, 2 * width * width, rows * width)
    out1, cross = pl.pallas_call(
        functools.partial(encoder_kernel, n),
        out_shape=(row_shape, jax.ShapeDtypeStruct((rows, 4 * HEAD), BF16)),
        in_specs=[SMEM] * 4 + [VMEM] + [ANY] * (3 + n),
        out_specs=(VMEM, VMEM),
        scratch_shapes=scratch
        + [
            pltpu.VMEM((3, width, 2 * HEAD), BF16),
            pltpu.SemaphoreType.DMA((3,)),
            pltpu.VMEM((rows, HEAD), BF16),
            pltpu.VMEM((rows, HEAD), BF16),
        ],
        compiler_params=params(),
        cost_estimate=layer_cost,
    )(section, row_order(), seq_lengths, scales, all_gains, full, kv_own, kv_other, *passed)
    cross2, cross3 = hop(cross[:, : 2 * HEAD], [(1, 2)]), hop(cross, [(1, 3)])

    result = pl.pallas_call(
        functools.partial(decoder_kernel, n),
        out_shape=row_shape,
        in_specs=[SMEM] * 3 + [VMEM, ANY, VMEM, VMEM, ANY, VMEM] + [ANY] * (2 * n),
        out_specs=VMEM,
        scratch_shapes=scratch + [pltpu.VMEM((rows, width), BF16)],
        compiler_params=params(),
        cost_estimate=layer_cost,
    )(section, seq_lengths, all_scales, wide_gain, full, cross2, cross3, out1, target2, *made, *passed)
    return result.reshape(1, micro, seqs, length, width), next_part[None]


def solution(mesh):
    in_specs = (
        P("section", "fsdp", None),
        P("section", "fsdp", None),
        P("section", None),
        P("section", None),
        P("section", None, "fsdp"),
        P(None, "fsdp", None, None),
        P(None, "fsdp", None, None),
        P(None, "fsdp"),
    )
    out_specs = (P("section", None, "fsdp", None, None), P("section", None, "fsdp"))
    return jax.shard_map(shards, mesh=mesh, in_specs=in_specs, out_specs=out_specs, check_vma=False)
```
